32 devices in a mesh: vox: 8 (over z, y), opt: 4 (over x, core).
Axes of the slice: x: 2, y: 2, z: 4, core: 2. Of those that a mesh axis runs over, the one named last changes fastest.
Arguments:
- source_fields: bfloat16 [1024, 6144], P('opt', 'vox'), may hold values from -6 to 6
- detector_fields: bfloat16 [4096, 6144], P('opt', 'vox'), may hold values from -6 to 6
- measured: float32 [1024, 4096], P('vox', 'opt'), may hold values from -6 to 6
- valid_pair: int32 [1024, 4096], P('vox', 'opt'), may hold values 0 or 1
- weight_class: int32 [1024, 4096], P('vox', 'opt'), may hold values from 0 to 3
- absorption: float32 [6144], P('vox'), may hold values from 0 to 1
Outputs:
- absorption_out: float32 [6144], P('vox')
- residual_out: float32 [1024, 4096], P('vox', 'opt')
The draws below stay inside these ranges and needn't reach their ends.
All inputs are finite; a program needn't handle non-finite values. No bound on the sum of `valid_pair` on one device may be relied on, other than what follows from the above.
Results may differ from the reference program's by a relative error of at most 0.0026.
Values may be sent and summed in bfloat16 or wider, within the bound.
A program may use at most 64 MiB of HBM per device.

```python
import jax
import jax.numpy as jnp
from jax import lax

NS = 1024
ND = 4096
ITERS = 2
VOXELS = 6144


def place_ends(drawn, rng, least, top_value):
    dims = drawn.shape
    index_at = [jax.random.randint(jax.random.fold_in(rng, axis), (), 0, dims[axis]) for axis in range(len(dims))]
    drawn = drawn.at[tuple(index_at)].set(least)
    longest = dims.index(max(dims))
    index_at[longest] = (index_at[longest] + 1) % dims[longest]
    return drawn.at[tuple(index_at)].set(top_value)


def raised(array, own_key, source, target, parts, factor):
    def block_of(position):
        return (jnp.arange(array.shape[position]) // (array.shape[position] // parts)).reshape((-1,) + (1,) * (array.ndim - 1 - position))

    first = jax.random.permutation(own_key, parts)[block_of(target)]
    other_side = (block_of(target) + parts // 2) % parts
    return jnp.where((block_of(source) == first) | (block_of(source) == other_side), factor * array, array)


def levels(rng, extent, pieces, least, high):
    factor_of = 1.0
    for dim, parts in pieces:
        steps = jax.random.uniform(jax.random.fold_in(jax.random.fold_in(rng, 6), dim), (parts,), jnp.float32, least / len(pieces), high / len(pieces))
        factor_of = factor_of * jnp.repeat(jnp.exp(steps), extent[dim] // parts).reshape((-1,) + (1,) * (len(extent) - 1 - dim))
    return factor_of


def centred(stream_key, shape, deviation, bound, shards=(), kind=jnp.bfloat16):
    drawn = jax.random.normal(stream_key, shape, jnp.float32) * deviation
    if len(shards) > 0:
        drawn = levels(stream_key, shape, shards, -0.22, 0.18) * drawn
    return jnp.clip(drawn, min=-bound, max=bound).astype(kind)


def noise_with(rng, extent, spread, most, shards, heavy, held_as=jnp.bfloat16):
    entries = spread * jax.random.normal(rng, extent, jnp.float32)
    if shards:
        entries = entries * levels(rng, extent, shards, -0.22, 0.18)
    return jnp.clip(raised(entries, jax.random.fold_in(rng, 3), *heavy), -most, most).astype(held_as)


def setup_inputs(seed: int = 0) -> dict:
    seeds = jax.random.split(jax.random.key(seed), 7)
    source_fields = noise_with(seeds[0], (NS, VOXELS), 1.0, 6.0, ((0, 4), (1, 8)), (1, 0, 8, 2.0))
    detector_fields = centred(seeds[1], (ND, VOXELS), 1.0, 6.0, ((0, 4), (1, 8)))
    measured = centred(seeds[2], (NS, ND), 1.0, 6.0, ((0, 8), (1, 4)), jnp.float32)
    valid_pair = place_ends((jax.random.randint(seeds[3], (NS, ND), 0, 4) < 3).astype(jnp.int32), jax.random.fold_in(seeds[3], 1), 0, 1)
    weight_class = place_ends(jax.random.randint(seeds[4], (NS, ND), 0, 4), jax.random.fold_in(seeds[4], 1), 0, 3).astype(jnp.int32)
    absorption = jnp.clip(1.0 * jax.random.uniform(seeds[5], (VOXELS,), jnp.float32) ** levels(seeds[5], (VOXELS,), ((0, 8),), -0.2, 0.2), 0.0, 1.0)
    return dict(source_fields=source_fields, detector_fields=detector_fields, measured=measured, valid_pair=valid_pair, weight_class=weight_class, absorption=absorption)


def reference(source_fields, detector_fields, measured, valid_pair, weight_class, absorption):
    voxels = source_fields.shape[1]
    pred_scale = 1.0 / jnp.sqrt(jnp.float32(voxels))
    grad_scale = jnp.sqrt(jnp.float32(voxels)) / (jnp.float32(NS) * jnp.float32(ND))
    maskf = valid_pair.astype(jnp.float32) / (1.0 + weight_class.astype(jnp.float32))
    mu_now = absorption
    weighted = jnp.zeros(measured.shape, jnp.float32)
    for step in range(ITERS):
        scaled = (detector_fields.astype(jnp.float32) * mu_now[None, :]).astype(jnp.bfloat16)
        predicted = lax.dot_general(source_fields, scaled, (((1,), (1,)), ((), ())), preferred_element_type=jnp.float32) * pred_scale
        weighted = maskf * (predicted - measured)
        weighted_b = weighted.astype(jnp.bfloat16)
        inner = jnp.dot(weighted_b, detector_fields, preferred_element_type=jnp.float32)
        gradient = lax.optimization_barrier(jnp.sum(inner * source_fields.astype(jnp.float32), axis=0)) * grad_scale
        mu_now = jnp.maximum(mu_now - 2.0 * gradient, 0.0)
    return (mu_now, weighted)
```

```python
import functools

import jax
import jax.numpy as jnp
import numpy as np
from jax import lax
from jax.experimental import pallas as pl
from jax.experimental.pallas import tpu as pltpu
from jax.sharding import PartitionSpec as P

ITERS = 2
MESH = pl.DeviceIdType.MESH


def kernel(
    A, B, NO, C, pred_scale, grad_scale,
    s_ref, d_ref, meas_ref, valid_ref, class_ref, mu_in,
    mu_ref, res_ref,
    s_full, maskf, scaled, ysend, yrecv, own, zsend, zrecv, wfull, gbuf,
    sx_send, sx_recv, sc_send, sc_recv, y_send, y_recv, z_send, z_recv,
    wz_send, wz_recv, wy_send, wy_recv, g_send, g_recv,
):
    q, R, X = s_ref.shape
    W = d_ref.shape[0] // C
    vox = lax.axis_index("vox")
    opt = lax.axis_index("opt")
    z, y = vox // B, lax.rem(vox, B)
    chip, core = opt // 2, lax.rem(opt, 2)
    NC = NO // 2
    mate = chip * 2 + 1 - core
    y_peers = [lax.rem(y + k, B) for k in range(1, B)]
    z_peers = [lax.rem(z + k, A) for k in range(1, A)]
    o_peers = [lax.rem(opt + k, NO) for k in range(1, NO)]
    c_peers = [lax.rem(chip + k, NC) for k in range(1, NC)]

    def at(zz, yy):
        return {"vox": zz * B + yy}

    barrier = pltpu.get_barrier_semaphore()
    for p in y_peers:
        pl.semaphore_signal(barrier, inc=1, device_id=at(z, p), device_id_type=MESH)
    for p in z_peers:
        pl.semaphore_signal(barrier, inc=1, device_id=at(p, y), device_id_type=MESH)
    for p in o_peers:
        pl.semaphore_signal(barrier, inc=1, device_id={"opt": p}, device_id_type=MESH)
    pl.semaphore_wait(barrier, A - 1 + B - 1 + NO - 1)

    def remote(src, dst, send, recv, where):
        return pltpu.make_async_remote_copy(
            src_ref=src, dst_ref=dst, send_sem=send, recv_sem=recv,
            device_id=where, device_id_type=MESH,
        )

    def block(j):
        return s_full.at[pl.ds(j * q, q)]

    def to_chip(p, j):
        return remote(s_ref, block(j), sx_send.at[p], sx_recv.at[j], {"opt": p * 2 + core})

    def to_mate(src, j):
        return remote(src, block(j), sc_send.at[j], sc_recv.at[j], {"opt": mate})

    for p in c_peers:
        to_chip(p, opt).start()
    to_mate(s_ref, opt).start()
    s_full[pl.ds(opt * q, q)] = s_ref[...]
    mu_ref[...] = mu_in[...]
    maskf[...] = valid_ref[...].astype(jnp.float32) / (1.0 + class_ref[...].astype(jnp.float32))
    for p in c_peers:
        to_chip(p, p * 2 + core).wait_recv()
        to_mate(block(p * 2 + core), p * 2 + core).start()
    for p in range(NC):
        to_mate(s_ref, p * 2 + 1 - core).wait_recv()
    for p in c_peers:
        to_chip(p, opt).wait_send()
        to_mate(s_ref, p * 2 + core).wait_send()
    to_mate(s_ref, opt).wait_send()

    def step(it, carry):
        def y_copy(c, p):
            return remote(
                ysend.at[c, p], yrecv.at[it, c, y], y_send.at[c, p], y_recv.at[it, c, y], at(z, p)
            )

        def z_copy(c, t, src):
            return remote(
                zsend.at[c, t], zrecv.at[it, c, src], z_send.at[c, t], z_recv.at[it, c, src], at(t, y)
            )

        def wz_copy(c, t, src):
            mine = wfull.at[it, c, src * B + y]
            return remote(mine, mine, wz_send.at[c, t], wz_recv.at[it, c, src], at(t, y))

        def wy_copy(c, src, p, yy):
            mine = wfull.at[it, c, src * B + yy]
            return remote(mine, mine, wy_send.at[c, src, p], wy_recv.at[it, c, src, yy], at(z, p))

        def rows_of(yy):
            return jnp.concatenate([s_full[a * B + yy] for a in range(A)], axis=0)

        def predict(c):
            scaled[...] = (
                d_ref[pl.ds(c * W, W)].astype(jnp.float32) * mu_ref[...]
            ).astype(jnp.bfloat16)

            def part(yy):
                return lax.dot_general(
                    rows_of(yy), scaled[...], (((1,), (1,)), ((), ())),
                    preferred_element_type=jnp.float32,
                ).reshape(A, R, W)

            for p in y_peers:
                ysend[c, p] = part(p).astype(jnp.bfloat16)
                y_copy(c, p).start()
            own[c] = part(y)

        def over_y(c):
            for p in y_peers:
                remote(
                    ysend.at[c, p], yrecv.at[it, c, p], y_send.at[c, p], y_recv.at[it, c, p], at(z, p)
                ).wait_recv()
            for t in z_peers:
                total = own[c, t]
                for p in y_peers:
                    total = total + yrecv[it, c, p, t].astype(jnp.float32)
                zsend[c, t] = total.astype(jnp.bfloat16)
                z_copy(c, t, z).start()

        def over_z(c):
            total = own[c, z]
            for p in y_peers:
                total = total + yrecv[it, c, p, z].astype(jnp.float32)
            for t in z_peers:
                z_copy(c, t, t).wait_recv()
                total = total + zrecv[it, c, t].astype(jnp.float32)
            cols = pl.ds(c * W, W)
            weighted = maskf[:, cols] * (total * pred_scale - meas_ref[:, cols])
            res_ref[:, cols] = weighted
            wfull[it, c, vox] = weighted.astype(jnp.bfloat16)
            for p in y_peers:
                wy_copy(c, z, p, y).start()
            for t in z_peers:
                wz_copy(c, t, z).start()

        def forward(c):
            for t in z_peers:
                wz_copy(c, t, t).wait_recv()
                for p in y_peers:
                    wy_copy(c, t, p, y).start()

        def gradient(c, total):
            for t in range(A):
                for p in y_peers:
                    wy_copy(c, t, p, p).wait_recv()
            d = d_ref[pl.ds(c * W, W)]

            def rows(a, total):
                w = wfull[it, c, pl.ds(a * B, B)].reshape(B * R, W)
                s = s_full[pl.ds(a * B, B)].reshape(B * R, X).astype(jnp.float32)
                inner = jnp.dot(w, d, preferred_element_type=jnp.float32) * s
                return total + jnp.sum(inner.reshape(B * R // 8, 8, X), axis=0)

            return lax.fori_loop(0, A, rows, total)

        for c in range(C):
            predict(c)
        total = jnp.zeros((8, X), jnp.float32)
        for slot in range(C + 4):
            if slot < C:
                over_y(slot)
            if 0 <= slot - 1 < C:
                over_z(slot - 1)
            if 0 <= slot - 2 < C:
                forward(slot - 2)
            if 0 <= slot - 3 < C:
                total = gradient(slot - 3, total)

        def g_copy(p, src):
            mine = gbuf.at[it, src]
            return remote(mine, mine, g_send.at[p], g_recv.at[it, src], {"opt": p})

        gbuf[it, opt] = total
        for p in o_peers:
            g_copy(p, opt).start()
        for c in range(C):
            for p in y_peers:
                y_copy(c, p).wait_send()
                for t in range(A):
                    wy_copy(c, t, p, y).wait_send()
            for t in z_peers:
                z_copy(c, t, z).wait_send()
                wz_copy(c, t, z).wait_send()
        for p in o_peers:
            g_copy(p, p).wait_recv()
        total = gbuf[it, 0]
        for j in range(1, NO):
            total = total + gbuf[it, j]
        grad = jnp.sum(total, axis=0, keepdims=True) * grad_scale
        mu_ref[...] = jnp.maximum(mu_ref[...] - 2.0 * grad, 0.0)
        for p in o_peers:
            g_copy(p, opt).wait_send()
        return carry

    lax.fori_loop(0, ITERS, step, 0)


def local(source_fields, detector_fields, measured, valid_pair, weight_class, absorption):
    NV, NO = lax.axis_size("vox"), lax.axis_size("opt")
    R, DL = measured.shape
    X = absorption.shape[0]
    q = source_fields.shape[0] // R
    B = 2
    A = NV // B
    W = min(DL, 256)
    C = DL // W
    pred_scale = float(np.float32(1.0) / np.sqrt(np.float32(X * NV)))
    grad_scale = float(np.sqrt(np.float32(X * NV)) / np.float32(R * NV * DL * NO))
    bf, f32 = jnp.bfloat16, jnp.float32
    dma = pltpu.SemaphoreType.DMA
    vmem = pl.BlockSpec(memory_space=pltpu.VMEM)
    mu, weighted = pl.pallas_call(
        functools.partial(kernel, A, B, NO, C, pred_scale, grad_scale),
        out_shape=(
            jax.ShapeDtypeStruct((1, X), f32),
            jax.ShapeDtypeStruct((R, DL), f32),
        ),
        in_specs=[vmem] * 6,
        out_specs=(vmem, vmem),
        scratch_shapes=[
            pltpu.VMEM((A * B, R, X), bf),
            pltpu.VMEM((R, DL), f32),
            pltpu.VMEM((W, X), bf),
            pltpu.VMEM((C, B, A, R, W), bf),
            pltpu.VMEM((ITERS, C, B, A, R, W), bf),
            pltpu.VMEM((C, A, R, W), f32),
            pltpu.VMEM((C, A, R, W), bf),
            pltpu.VMEM((ITERS, C, A, R, W), bf),
            pltpu.VMEM((ITERS, C, A * B, R, W), bf),
            pltpu.VMEM((ITERS, NO, 8, X), f32),
            dma((NO // 2,)), dma((NO,)), dma((NO,)), dma((NO,)),
            dma((C, B)), dma((ITERS, C, B)),
            dma((C, A)), dma((ITERS, C, A)),
            dma((C, A)), dma((ITERS, C, A)),
            dma((C, A, B)), dma((ITERS, C, A, B)),
            dma((NO,)), dma((ITERS, NO)),
        ],
        compiler_params=pltpu.CompilerParams(
            collective_id=0, has_side_effects=True, vmem_limit_bytes=52 * 1024 * 1024
        ),
    )(
        source_fields.reshape(q, R, X), detector_fields, measured, valid_pair, weight_class,
        absorption.reshape(1, X),
    )
    return mu.reshape(X), weighted


def solution(mesh):
    placed = (
        P("opt", "vox"),
        P("opt", "vox"),
        P("vox", "opt"),
        P("vox", "opt"),
        P("vox", "opt"),
        P("vox"),
    )
    return jax.shard_map(
        local, mesh=mesh, in_specs=placed, out_specs=(P("vox"), P("vox", "opt")), check_vma=False
    )
```

```python
import functools

import jax
import jax.numpy as jnp
import numpy as np
from jax import lax
from jax.experimental import pallas as pl
from jax.experimental.pallas import tpu as pltpu
from jax.sharding import PartitionSpec as P

ITERS = 2
MESH = pl.DeviceIdType.MESH


def kernel(
    A, B, NO, C, pred_scale, grad_scale,
    s_ref, d_in, meas_in, valid_in, class_in, mu_in,
    mu_ref, res_ref,
    d_ref, meas_ref, valid_ref, class_ref, s_full, maskf, scaled, ysend, yrecv, own, zsend, zrecv, wfull, gbuf,
    sx_send, sx_recv, sc_send, sc_recv, y_send, y_recv, z_send, z_recv,
    wz_send, wz_recv, wy_send, wy_recv, g_send, g_recv, in_sem,
):
    q, R, X = s_ref.shape
    W = d_ref.shape[0] // C
    vox = lax.axis_index("vox")
    opt = lax.axis_index("opt")
    z, y = vox // B, lax.rem(vox, B)
    chip, core = opt // 2, lax.rem(opt, 2)
    NC = NO // 2
    mate = chip * 2 + 1 - core
    y_peers = [lax.rem(y + k, B) for k in range(1, B)]
    up, down = z + 1, z - 1
    z_peers = [lax.rem(z + k, A) for k in range(1, A)]
    o_peers = [lax.rem(opt + k, NO) for k in range(1, NO)]
    c_peers = [lax.rem(chip + k, NC) for k in range(1, NC)]

    def y_first(c):
        return c % 2 == 1

    def at(zz, yy):
        return {"vox": zz * B + yy}

    loads = [
        pltpu.make_async_copy(valid_in, valid_ref, in_sem.at[0]),
        pltpu.make_async_copy(class_in, class_ref, in_sem.at[1]),
        pltpu.make_async_copy(s_ref, s_full.at[pl.ds(opt * q, q)], in_sem.at[2]),
        pltpu.make_async_copy(d_in, d_ref, in_sem.at[3]),
        pltpu.make_async_copy(meas_in, meas_ref, in_sem.at[4]),
    ]
    for load in loads:
        load.start()

    barrier = pltpu.get_barrier_semaphore()
    for p in y_peers:
        pl.semaphore_signal(barrier, inc=1, device_id=at(z, p), device_id_type=MESH)
    for p in z_peers:
        pl.semaphore_signal(barrier, inc=1, device_id=at(p, y), device_id_type=MESH)
    for p in o_peers:
        pl.semaphore_signal(barrier, inc=1, device_id={"opt": p}, device_id_type=MESH)
    pl.semaphore_wait(barrier, A - 1 + B - 1 + NO - 1)

    def remote(src, dst, send, recv, where):
        return pltpu.make_async_remote_copy(
            src_ref=src, dst_ref=dst, send_sem=send, recv_sem=recv,
            device_id=where, device_id_type=MESH,
        )

    def block(j):
        return s_full.at[pl.ds(j * q, q)]

    def to_chip(p, j):
        return remote(s_ref, block(j), sx_send.at[p], sx_recv.at[j], {"opt": p * 2 + core})

    def to_mate(src, j):
        return remote(src, block(j), sc_send.at[j], sc_recv.at[j], {"opt": mate})

    for p in c_peers:
        to_chip(p, opt).start()
    to_mate(s_ref, opt).start()
    for load in loads:
        load.wait()
    mu_ref[...] = mu_in[...]
    maskf[...] = valid_ref[...].astype(jnp.float32) / (1.0 + class_ref[...].astype(jnp.float32))
    for p in c_peers:
        to_chip(p, p * 2 + core).wait_recv()
        to_mate(block(p * 2 + core), p * 2 + core).start()
    for p in range(NC):
        to_mate(s_ref, p * 2 + 1 - core).wait_recv()
    for p in c_peers:
        to_chip(p, opt).wait_send()
        to_mate(s_ref, p * 2 + core).wait_send()
    to_mate(s_ref, opt).wait_send()

    def step(it, carry):
        def y_copy(c, p):
            return remote(
                ysend.at[c, p], yrecv.at[it, c, y], y_send.at[c, p], y_recv.at[it, c, y], at(z, p)
            )

        def z_copy(c, t, src):
            return remote(
                zsend.at[c, t], zrecv.at[it, c, src], z_send.at[c, t], z_recv.at[it, c, src], at(t, y)
            )

        def wz_copy(c, src, yy, way):
            mine = wfull.at[it, c, src * B + yy]
            return remote(
                mine, mine, wz_send.at[c, src, yy, way], wz_recv.at[it, c, src, yy],
                at(up if way else down, y),
            )

        def can(way):
            return z < A - 1 if way else z > 0

        def spread(c, yy):
            for way in (0, 1):
                @pl.when(can(way))
                def _():
                    wz_copy(c, z, yy, way).start()

        def columns(c):
            return [y] + y_peers if y_first(c) else [y]

        def wy_copy(c, src, p, yy):
            mine = wfull.at[it, c, src * B + yy]
            return remote(mine, mine, wy_send.at[c, src, p], wy_recv.at[it, c, src, yy], at(z, p))

        def rows_of(yy):
            return jnp.concatenate([s_full[a * B + yy] for a in range(A)], axis=0)

        def predict(c):
            scaled[...] = (
                d_ref[pl.ds(c * W, W)].astype(jnp.float32) * mu_ref[...]
            ).astype(jnp.bfloat16)

            def part(yy):
                return lax.dot_general(
                    rows_of(yy), scaled[...], (((1,), (1,)), ((), ())),
                    preferred_element_type=jnp.float32,
                ).reshape(A, R, W)

            for p in y_peers:
                ysend[c, p] = part(p).astype(jnp.bfloat16)
            if c == 0:
                send_y(c)
            own[c] = part(y)

        def send_y(c):
            for p in y_peers:
                y_copy(c, p).start()

        def over_y(c):
            for p in y_peers:
                remote(
                    ysend.at[c, p], yrecv.at[it, c, p], y_send.at[c, p], y_recv.at[it, c, p], at(z, p)
                ).wait_recv()
            if c + 1 < C:
                send_y(c + 1)
            for t in z_peers:
                total = own[c, t]
                for p in y_peers:
                    total = total + yrecv[it, c, p, t].astype(jnp.float32)
                zsend[c, t] = total.astype(jnp.bfloat16)
                z_copy(c, t, z).start()

        def over_z(c):
            total = own[c, z]
            for p in y_peers:
                total = total + yrecv[it, c, p, z].astype(jnp.float32)
            for t in z_peers:
                z_copy(c, t, t).wait_recv()
                total = total + zrecv[it, c, t].astype(jnp.float32)
            cols = pl.ds(c * W, W)
            weighted = maskf[:, cols] * (total * pred_scale - meas_ref[:, cols])
            res_ref[:, cols] = weighted
            wfull[it, c, vox] = weighted.astype(jnp.bfloat16)
            for p in y_peers:
                wy_copy(c, z, p, y).start()
            spread(c, y)

        def forward(c):
            if y_first(c):
                for p in y_peers:
                    wy_copy(c, z, p, p).wait_recv()
                    spread(c, p)
            for k in range(1, A):
                for way in (0, 1):
                    src = z - k if way else z + k

                    @pl.when(src >= 0 if way else src < A)
                    def _():
                        for yy in columns(c):
                            wz_copy(c, src, yy, way).wait_recv()

                            @pl.when(can(way))
                            def _():
                                wz_copy(c, src, yy, way).start()

                        if not y_first(c):
                            for p in y_peers:
                                wy_copy(c, src, p, y).start()

        def sent(c):
            for p in y_peers:
                y_copy(c, p).wait_send()
                for src in [z] if y_first(c) else range(A):
                    wy_copy(c, src, p, y).wait_send()
            for t in z_peers:
                z_copy(c, t, z).wait_send()
            for k in range(A):
                for way in (0, 1):
                    src = z - k if way else z + k

                    @pl.when(jnp.logical_and(src >= 0 if way else src < A, can(way)))
                    def _():
                        for yy in columns(c):
                            wz_copy(c, src, yy, way).wait_send()

        def gradient(c, total):
            if not y_first(c):
                for t in range(A):
                    for p in y_peers:
                        wy_copy(c, t, p, p).wait_recv()
            d = d_ref[pl.ds(c * W, W)]

            def rows(a, total):
                w = wfull[it, c, pl.ds(a * B, B)].reshape(B * R, W)
                s = s_full[pl.ds(a * B, B)].reshape(B * R, X).astype(jnp.float32)
                inner = jnp.dot(w, d, preferred_element_type=jnp.float32) * s
                return total + jnp.sum(inner.reshape(B * R // 8, 8, X), axis=0)

            return lax.fori_loop(0, A, rows, total)

        predict(0)
        if C > 1:
            predict(1)
        total = jnp.zeros((8, X), jnp.float32)
        for slot in range(C + 4):
            if slot < C:
                over_y(slot)
            if slot + 2 < C:
                predict(slot + 2)
            if 0 <= slot - 1 < C:
                over_z(slot - 1)
            if 0 <= slot - 2 < C:
                forward(slot - 2)
            if 0 <= slot - 3 < C:
                total = gradient(slot - 3, total)

        def g_copy(p, src):
            mine = gbuf.at[it, src]
            return remote(mine, mine, g_send.at[p], g_recv.at[it, src], {"opt": p})

        gbuf[it, opt] = total
        for p in o_peers:
            g_copy(p, opt).start()
        for c in range(C):
            sent(c)
        for p in o_peers:
            g_copy(p, p).wait_recv()
        total = gbuf[it, 0]
        for j in range(1, NO):
            total = total + gbuf[it, j]
        grad = jnp.sum(total, axis=0, keepdims=True) * grad_scale
        mu_ref[...] = jnp.maximum(mu_ref[...] - 2.0 * grad, 0.0)
        for p in o_peers:
            g_copy(p, opt).wait_send()
        return carry

    lax.fori_loop(0, ITERS, step, 0)


def local(source_fields, detector_fields, measured, valid_pair, weight_class, absorption):
    NV, NO = lax.axis_size("vox"), lax.axis_size("opt")
    R, DL = measured.shape
    X = absorption.shape[0]
    q = source_fields.shape[0] // R
    B = 2
    A = NV // B
    W = min(DL, 256)
    C = DL // W
    pred_scale = float(np.float32(1.0) / np.sqrt(np.float32(X * NV)))
    grad_scale = float(np.sqrt(np.float32(X * NV)) / np.float32(R * NV * DL * NO))
    bf, f32 = jnp.bfloat16, jnp.float32
    dma = pltpu.SemaphoreType.DMA
    vmem = pl.BlockSpec(memory_space=pltpu.VMEM)
    mu, weighted = pl.pallas_call(
        functools.partial(kernel, A, B, NO, C, pred_scale, grad_scale),
        out_shape=(
            jax.ShapeDtypeStruct((1, X), f32),
            jax.ShapeDtypeStruct((R, DL), f32),
        ),
        in_specs=[pl.BlockSpec(memory_space=pl.ANY)] * 5 + [vmem],
        out_specs=(vmem, vmem),
        scratch_shapes=[
            pltpu.VMEM((DL, X), bf),
            pltpu.VMEM((R, DL), f32),
            pltpu.VMEM((R, DL), jnp.int32),
            pltpu.VMEM((R, DL), jnp.int32),
            pltpu.VMEM((A * B, R, X), bf),
            pltpu.VMEM((R, DL), f32),
            pltpu.VMEM((W, X), bf),
            pltpu.VMEM((C, B, A, R, W), bf),
            pltpu.VMEM((ITERS, C, B, A, R, W), bf),
            pltpu.VMEM((C, A, R, W), f32),
            pltpu.VMEM((C, A, R, W), bf),
            pltpu.VMEM((ITERS, C, A, R, W), bf),
            pltpu.VMEM((ITERS, C, A * B, R, W), bf),
            pltpu.VMEM((ITERS, NO, 8, X), f32),
            dma((NO // 2,)), dma((NO,)), dma((NO,)), dma((NO,)),
            dma((C, B)), dma((ITERS, C, B)),
            dma((C, A)), dma((ITERS, C, A)),
            dma((C, A, B, 2)), dma((ITERS, C, A, B)),
            dma((C, A, B)), dma((ITERS, C, A, B)),
            dma((NO,)), dma((ITERS, NO)),
            dma((5,)),
        ],
        compiler_params=pltpu.CompilerParams(
            collective_id=0, has_side_effects=True, vmem_limit_bytes=52 * 1024 * 1024
        ),
    )(
        source_fields.reshape(q, R, X), detector_fields, measured, valid_pair, weight_class,
        absorption.reshape(1, X),
    )
    return mu.reshape(X), weighted


def solution(mesh):
    placed = (
        P("opt", "vox"),
        P("opt", "vox"),
        P("vox", "opt"),
        P("vox", "opt"),
        P("vox", "opt"),
        P("vox"),
    )
    return jax.shard_map(
        local, mesh=mesh, in_specs=placed, out_specs=(P("vox"), P("vox", "opt")), check_vma=False
    )
```

```python
import functools

import jax
import jax.numpy as jnp
import numpy as np
from jax import lax
from jax.experimental import pallas as pl
from jax.experimental.pallas import tpu as pltpu
from jax.sharding import PartitionSpec as P

ITERS = 2
MESH = pl.DeviceIdType.MESH


def kernel(
    A, B, NO, W, pred_scale, grad_scale,
    s_in, d_in, meas_in, valid_in, class_in, mu_in,
    mu_out, res_ref,
    s_full, d_full, meas_ref, valid_ref, class_ref, codes, code_ref, mu_ref, scaled,
    own, zsend, zrecv, wfull, rsend, rrecv, gbuf,
    sy_send, sy_recv, sx_send, sx_recv, sm_send, sm_recv, d_send, d_recv,
    p_send, p_recv, r_send, r_recv, z_send, z_recv, w_send, w_recv, g_send, g_recv, in_sem,
):
    q, R, X = s_in.shape
    H = d_in.shape[0] // B
    NH = H // W
    C = NH * B
    vox = lax.axis_index("vox")
    opt = lax.axis_index("opt")
    z, y = vox // B, lax.rem(vox, B)
    chip, core = opt // 2, lax.rem(opt, 2)
    NC = NO // 2
    mate = chip * 2 + 1 - core
    rows_y = [lax.rem(y + k, B) for k in range(B)]
    y_peers = rows_y[1:]
    z_peers = [lax.rem(z + k, A) for k in range(1, A)]
    c_peers = [lax.rem(chip + k, NC) for k in range(1, NC)]
    group = [
        (lax.rem(y + k, B), lax.rem(opt + j, NO)) for k in range(B) for j in range(NO) if k + j > 0
    ]

    def remote(src, dst, send, recv, where):
        return pltpu.make_async_remote_copy(
            src_ref=src, dst_ref=dst, send_sem=send, recv_sem=recv,
            device_id=where, device_id_type=MESH,
        )

    def half(yy):
        return pl.ds(pl.multiple_of(yy * X, X), X)

    def cols(yy):
        return pl.ds(pl.multiple_of(yy * H, H), H)

    def at_y(p):
        return {"vox": z * B + p}

    def at_z(t):
        return {"vox": t * B + y}

    def block(j, yy):
        return s_full.at[pl.ds(j * q, q), :, half(yy)]

    def d_block(h, yy):
        return d_full.at[pl.ds(h * W, W), half(yy)]

    def d_rows(h, yy):
        return d_in.at[pl.ds(pl.multiple_of(yy * H + h * W, W), W)]

    loads = [
        pltpu.make_async_copy(valid_in, valid_ref, in_sem.at[0]),
        pltpu.make_async_copy(class_in, class_ref, in_sem.at[1]),
        pltpu.make_async_copy(s_in, block(opt, y), in_sem.at[2]),
        pltpu.make_async_copy(meas_in.at[:, cols(y)], meas_ref.at[y], in_sem.at[3]),
    ] + [
        pltpu.make_async_copy(d_rows(h, y), d_block(h, y), in_sem.at[4 + h]) for h in range(NH)
    ]
    for load in loads:
        load.start()

    barrier = pltpu.get_barrier_semaphore()
    for t in z_peers:
        pl.semaphore_signal(barrier, inc=1, device_id=at_z(t), device_id_type=MESH)
    for p, j in group:
        pl.semaphore_signal(
            barrier, inc=1, device_id={"vox": z * B + p, "opt": j}, device_id_type=MESH
        )
    pl.semaphore_wait(barrier, A - 1 + B * NO - 1)

    def s_y(p, yy):
        return remote(s_in, block(opt, yy), sy_send.at[p], sy_recv.at[yy], at_y(p))

    def s_x(p, j, yy):
        return remote(
            block(j, yy), block(j, yy), sx_send.at[p, yy], sx_recv.at[j // 2, yy],
            {"opt": p * 2 + core},
        )

    def s_x_own(p):
        return remote(
            s_in, block(opt, y), sx_send.at[p, y], sx_recv.at[chip, y], {"opt": p * 2 + core}
        )

    def s_m(p, cc, yy):
        mine = block(p * 2 + cc, yy)
        return remote(mine, mine, sm_send.at[p, yy], sm_recv.at[p, yy], {"opt": mate})

    def s_m_own():
        return remote(s_in, block(opt, y), sm_send.at[chip, y], sm_recv.at[chip, y], {"opt": mate})

    def d_y(h, p, yy):
        return remote(d_rows(h, p), d_block(h, yy), d_send.at[h, p], d_recv.at[h, yy], at_y(p))

    def pairs(p, yy):
        return [
            remote(mu_in, mu_ref.at[:, half(yy)], p_send.at[0, p], p_recv.at[0, yy], at_y(p)),
            remote(
                meas_in.at[:, cols(p)], meas_ref.at[yy], p_send.at[1, p], p_recv.at[1, yy], at_y(p)
            ),
            remote(
                codes.at[:, cols(p)], code_ref.at[yy], p_send.at[2, p], p_recv.at[2, yy], at_y(p)
            ),
        ]

    for p in y_peers:
        s_y(p, y).start()
    for p in c_peers:
        s_x_own(p).start()
    s_m_own().start()
    for p in y_peers:
        pairs(p, y)[0].start()
    for load in loads:
        load.wait()
    mu_ref[:, half(y)] = mu_in[...]
    codes[...] = (valid_ref[...] * (1 + class_ref[...])).astype(jnp.float32).astype(jnp.bfloat16)
    code_ref[y] = codes[:, cols(y)]
    for p in y_peers:
        s_y(p, p).wait_recv()
        d_y(0, p, y).start()
        for pp in c_peers:
            s_x(pp, opt, p).start()
        s_m(chip, core, p).start()
    for yy in rows_y:
        for p in c_peers:
            s_x(p, p * 2 + core, yy).wait_recv()
            s_m(p, core, yy).start()
    for p in y_peers:
        for copy in pairs(p, y)[1:]:
            copy.start()
        for h in range(1, NH):
            d_y(h, p, y).start()
    for yy in rows_y:
        for p in range(NC):
            s_m(p, 1 - core, yy).wait_recv()
    for p in y_peers:
        pairs(p, p)[0].wait_recv()
        s_y(p, y).wait_send()
    for p in c_peers:
        s_x_own(p).wait_send()
        for yy in y_peers:
            s_x(p, opt, yy).wait_send()
    for p in range(NC):
        for yy in rows_y:
            s_m(p, core, yy).wait_send()

    def back(h, p, yy):
        return remote(
            rsend.at[h, p], rrecv.at[h, yy], r_send.at[h, p], r_recv.at[h, yy], at_y(p)
        )

    def step(it, carry):
        def z_copy(c, t, src):
            return remote(
                zsend.at[c, t], zrecv.at[it, c, src], z_send.at[c, t], z_recv.at[it, c, src], at_z(t)
            )

        def w_copy(c, t, src):
            mine = wfull.at[it, c, src]
            return remote(mine, mine, w_send.at[c, t], w_recv.at[it, c, src], at_z(t))

        def predict(c):
            h, r = c // B, rows_y[c % B]
            if c % B == 0:
                @pl.when(it == 0)
                def _():
                    for p in y_peers:
                        d_y(h, p, p).wait_recv()

                scaled[...] = (
                    d_full[pl.ds(h * W, W)].astype(jnp.float32) * mu_ref[...]
                ).astype(jnp.bfloat16)
            rows = jnp.concatenate([s_full[a * B + r] for a in range(A)], axis=0)
            part = lax.dot_general(
                rows, scaled[...], (((1,), (1,)), ((), ())), preferred_element_type=jnp.float32
            ).reshape(A, R, W)
            zsend[c] = part.astype(jnp.bfloat16)
            for t in z_peers:
                z_copy(c, t, z).start()
            own[c] = part

        def over_z(c):
            h, k = c // B, c % B
            r = rows_y[k]
            if h == 0 and k > 0:
                @pl.when(it == 0)
                def _():
                    for copy in pairs(r, r)[1:]:
                        copy.wait_recv()

            total = own[c, z]
            for t in z_peers:
                z_copy(c, t, t).wait_recv()
                total = total + zrecv[it, c, t].astype(jnp.float32)
            here = pl.ds(h * W, W)
            code = code_ref[r, :, here].astype(jnp.float32)
            weight = jnp.where(code > 0.0, 1.0 / jnp.maximum(code, 1.0), 0.0)
            weighted = weight * (total * pred_scale - meas_ref[r, :, here])
            wfull[it, c, z] = weighted.astype(jnp.bfloat16)
            for t in z_peers:
                w_copy(c, t, z).start()
            rsend[h, r] = weighted
            if k > 0:
                @pl.when(it == ITERS - 1)
                def _():
                    back(h, r, y).start()

        def gradient(c, total):
            h, r = c // B, rows_y[c % B]
            for t in z_peers:
                w_copy(c, t, t).wait_recv()
            d = d_full[pl.ds(h * W, W)]

            def rows(i, total):
                w = wfull[it, c, pl.ds(2 * i, 2)].reshape(2 * R, W)
                s = jnp.concatenate([s_full[(2 * i + k) * B + r] for k in range(2)], axis=0)
                inner = jnp.dot(w, d, preferred_element_type=jnp.float32) * s.astype(jnp.float32)
                return total + jnp.sum(inner.reshape(2 * R // 8, 8, B * X), axis=0)

            return lax.fori_loop(0, A // 2, rows, total)

        total = jnp.zeros((8, B * X), jnp.float32)
        for c in range(min(2, C)):
            predict(c)
        for slot in range(C + 1):
            if slot + 2 < C:
                predict(slot + 2)
            if slot < C:
                over_z(slot)
            if slot > 0:
                total = gradient(slot - 1, total)

        def g_copy(p, j, sp, sj):
            mine = gbuf.at[it, sp * NO + sj]
            return remote(
                mine, mine, g_send.at[p * NO + j], g_recv.at[it, sp * NO + sj],
                {"vox": z * B + p, "opt": j},
            )

        gbuf[it, y * NO + opt] = jnp.sum(total, axis=0, keepdims=True)
        for p, j in group:
            g_copy(p, j, y, opt).start()
        for c in range(C):
            for t in z_peers:
                z_copy(c, t, z).wait_send()
                w_copy(c, t, z).wait_send()
        for p, j in group:
            g_copy(p, j, p, j).wait_recv()
        grad = gbuf[it, 0]
        for j in range(1, B * NO):
            grad = grad + gbuf[it, j]
        mu_ref[...] = jnp.maximum(mu_ref[...] - 2.0 * (grad * grad_scale), 0.0)
        for p, j in group:
            g_copy(p, j, y, opt).wait_send()
        return carry

    lax.fori_loop(0, ITERS, step, 0)
    mu_out[...] = mu_ref[:, half(y)]
    for h in range(NH):
        res_ref[:, pl.ds(pl.multiple_of(y * H + h * W, W), W)] = rsend[h, y]
        for p in y_peers:
            back(h, p, p).wait_recv()
            res_ref[:, pl.ds(pl.multiple_of(p * H + h * W, W), W)] = rrecv[h, p]
            back(h, p, y).wait_send()
            d_y(h, p, y).wait_send()
    for p in y_peers:
        for copy in pairs(p, y):
            copy.wait_send()


def local(source_fields, detector_fields, measured, valid_pair, weight_class, absorption):
    NV, NO = lax.axis_size("vox"), lax.axis_size("opt")
    R, DL = measured.shape
    X = absorption.shape[0]
    q = source_fields.shape[0] // R
    B = 2 if DL % 256 == 0 and NV % 4 == 0 else 1
    A = NV // B
    H = DL // B
    W = min(H, 256)
    NH = H // W
    C = NH * B
    pred_scale = float(np.float32(1.0) / np.sqrt(np.float32(X * NV)))
    grad_scale = float(np.sqrt(np.float32(X * NV)) / np.float32(R * NV * DL * NO))
    bf, f32 = jnp.bfloat16, jnp.float32
    dma = pltpu.SemaphoreType.DMA
    vmem = pl.BlockSpec(memory_space=pltpu.VMEM)
    mu, weighted = pl.pallas_call(
        functools.partial(kernel, A, B, NO, W, pred_scale, grad_scale),
        out_shape=(
            jax.ShapeDtypeStruct((1, X), f32),
            jax.ShapeDtypeStruct((R, DL), f32),
        ),
        in_specs=[pl.BlockSpec(memory_space=pl.ANY)] * 5 + [vmem],
        out_specs=(vmem, vmem),
        scratch_shapes=[
            pltpu.VMEM((A * B, R, B * X), bf),
            pltpu.VMEM((H, B * X), bf),
            pltpu.VMEM((B, R, H), f32),
            pltpu.VMEM((R, DL), jnp.int32),
            pltpu.VMEM((R, DL), jnp.int32),
            pltpu.VMEM((R, DL), bf),
            pltpu.VMEM((B, R, H), bf),
            pltpu.VMEM((1, B * X), f32),
            pltpu.VMEM((W, B * X), bf),
            pltpu.VMEM((C, A, R, W), f32),
            pltpu.VMEM((C, A, R, W), bf),
            pltpu.VMEM((ITERS, C, A, R, W), bf),
            pltpu.VMEM((ITERS, C, A, R, W), bf),
            pltpu.VMEM((NH, B, R, W), f32),
            pltpu.VMEM((NH, B, R, W), f32),
            pltpu.VMEM((ITERS, B * NO, 1, B * X), f32),
            dma((B,)), dma((B,)),
            dma((NO // 2, B)), dma((NO // 2, B)),
            dma((NO // 2, B)), dma((NO // 2, B)),
            dma((NH, B)), dma((NH, B)),
            dma((3, B)), dma((3, B)),
            dma((NH, B)), dma((NH, B)),
            dma((C, A)), dma((ITERS, C, A)),
            dma((C, A)), dma((ITERS, C, A)),
            dma((B * NO,)), dma((ITERS, B * NO)),
            dma((4 + NH,)),
        ],
        compiler_params=pltpu.CompilerParams(
            collective_id=0, has_side_effects=True, vmem_limit_bytes=52 * 1024 * 1024
        ),
    )(
        source_fields.reshape(q, R, X), detector_fields, measured, valid_pair, weight_class,
        absorption.reshape(1, X),
    )
    return mu.reshape(X), weighted


def solution(mesh):
    placed = (
        P("opt", "vox"),
        P("opt", "vox"),
        P("vox", "opt"),
        P("vox", "opt"),
        P("vox", "opt"),
        P("vox"),
    )
    return jax.shard_map(
        local, mesh=mesh, in_specs=placed, out_specs=(P("vox"), P("vox", "opt")), check_vma=False
    )
```

```python
import functools

import jax
import jax.numpy as jnp
import numpy as np
from jax import lax
from jax.experimental import pallas as pl
from jax.experimental.pallas import tpu as pltpu
from jax.sharding import PartitionSpec as P

ITERS = 2
MESH = pl.DeviceIdType.MESH


def kernel(
    A, B, NO, W, pred_scale, grad_scale,
    s_in, d_in, meas_in, valid_in, class_in, mu_in,
    mu_out, res_ref,
    s_full, d_full, meas_ref, valid_ref, class_ref, codes, code_ref, mu_ref, scaled,
    own, zsend, zrecv, zrel, wfull, rsend, rrecv, gbuf,
    sy_send, sy_recv, sx_send, sx_recv, sm_send, sm_recv, d_send, d_recv,
    p_send, p_recv, r_send, r_recv, z_send, z_recv, rel_recv, w_send, w_recv, g_send, g_recv, in_sem,
):
    q, R, X = s_in.shape
    H = d_in.shape[0] // B
    NH = H // W
    C = NH * B
    vox = lax.axis_index("vox")
    opt = lax.axis_index("opt")
    z, y = vox // B, lax.rem(vox, B)
    chip, core = opt // 2, lax.rem(opt, 2)
    NC = NO // 2
    mate = chip * 2 + 1 - core
    rows_y = [lax.rem(y + k, B) for k in range(B)]
    y_peers = rows_y[1:]
    z_peers = [lax.rem(z + k, A) for k in range(1, A)]
    line = A == 4
    inner = lax.rem((z + 1) // 2, 2)
    near = inner * 3 * (z - 1) + (1 - inner) * (1 + z // 3)
    far = inner * 3 * (2 - z) + (1 - inner) * (3 - z)
    c_peers = [lax.rem(chip + k, NC) for k in range(1, NC)]
    group = [
        (lax.rem(y + k, B), lax.rem(opt + j, NO)) for k in range(B) for j in range(NO) if k + j > 0
    ]

    def remote(src, dst, send, recv, where):
        return pltpu.make_async_remote_copy(
            src_ref=src, dst_ref=dst, send_sem=send, recv_sem=recv,
            device_id=where, device_id_type=MESH,
        )

    def half(yy):
        return pl.ds(pl.multiple_of(yy * X, X), X)

    def cols(yy):
        return pl.ds(pl.multiple_of(yy * H, H), H)

    def at_y(p):
        return {"vox": z * B + p}

    def at_z(t):
        return {"vox": t * B + y}

    def block(j, yy):
        return s_full.at[pl.ds(j * q, q), :, half(yy)]

    def d_block(h, yy):
        return d_full.at[pl.ds(h * W, W), half(yy)]

    def d_rows(h, yy):
        return d_in.at[pl.ds(pl.multiple_of(yy * H + h * W, W), W)]

    loads = [
        pltpu.make_async_copy(valid_in, valid_ref, in_sem.at[0]),
        pltpu.make_async_copy(class_in, class_ref, in_sem.at[1]),
        pltpu.make_async_copy(s_in, block(opt, y), in_sem.at[2]),
        pltpu.make_async_copy(meas_in.at[:, cols(y)], meas_ref.at[y], in_sem.at[3]),
    ] + [
        pltpu.make_async_copy(d_rows(h, y), d_block(h, y), in_sem.at[4 + h]) for h in range(NH)
    ]
    for load in loads:
        load.start()

    barrier = pltpu.get_barrier_semaphore()
    for t in z_peers:
        pl.semaphore_signal(barrier, inc=1, device_id=at_z(t), device_id_type=MESH)
    for p, j in group:
        pl.semaphore_signal(
            barrier, inc=1, device_id={"vox": z * B + p, "opt": j}, device_id_type=MESH
        )
    pl.semaphore_wait(barrier, A - 1 + B * NO - 1)

    def s_y(p, yy):
        return remote(s_in, block(opt, yy), sy_send.at[p], sy_recv.at[yy], at_y(p))

    def s_x(p, j, yy):
        return remote(
            block(j, yy), block(j, yy), sx_send.at[p, yy], sx_recv.at[j // 2, yy],
            {"opt": p * 2 + core},
        )

    def s_x_own(p):
        return remote(
            s_in, block(opt, y), sx_send.at[p, y], sx_recv.at[chip, y], {"opt": p * 2 + core}
        )

    def s_m(p, cc, yy):
        mine = block(p * 2 + cc, yy)
        return remote(mine, mine, sm_send.at[p, yy], sm_recv.at[p, yy], {"opt": mate})

    def s_m_own():
        return remote(s_in, block(opt, y), sm_send.at[chip, y], sm_recv.at[chip, y], {"opt": mate})

    def d_y(h, p, yy):
        return remote(d_rows(h, p), d_block(h, yy), d_send.at[h, p], d_recv.at[h, yy], at_y(p))

    def pairs(p, yy):
        return [
            remote(mu_in, mu_ref.at[:, half(yy)], p_send.at[0, p], p_recv.at[0, yy], at_y(p)),
            remote(
                meas_in.at[:, cols(p)], meas_ref.at[yy], p_send.at[1, p], p_recv.at[1, yy], at_y(p)
            ),
            remote(
                codes.at[:, cols(p)], code_ref.at[yy], p_send.at[2, p], p_recv.at[2, yy], at_y(p)
            ),
        ]

    for p in y_peers:
        s_y(p, y).start()
    for p in c_peers:
        s_x_own(p).start()
    s_m_own().start()
    for p in y_peers:
        pairs(p, y)[0].start()
    for load in loads:
        load.wait()
    mu_ref[:, half(y)] = mu_in[...]
    codes[...] = (valid_ref[...] * (1 + class_ref[...])).astype(jnp.float32).astype(jnp.bfloat16)
    code_ref[y] = codes[:, cols(y)]
    for p in y_peers:
        s_y(p, p).wait_recv()
        d_y(0, p, y).start()
        for pp in c_peers:
            s_x(pp, opt, p).start()
        s_m(chip, core, p).start()
    for yy in rows_y:
        for p in c_peers:
            s_x(p, p * 2 + core, yy).wait_recv()
            s_m(p, core, yy).start()
    for p in y_peers:
        for copy in pairs(p, y)[1:]:
            copy.start()
        for h in range(1, NH):
            d_y(h, p, y).start()
    for yy in rows_y:
        for p in range(NC):
            s_m(p, 1 - core, yy).wait_recv()
    for p in y_peers:
        pairs(p, p)[0].wait_recv()
        s_y(p, y).wait_send()
    for p in c_peers:
        s_x_own(p).wait_send()
        for yy in y_peers:
            s_x(p, opt, yy).wait_send()
    for p in range(NC):
        for yy in rows_y:
            s_m(p, core, yy).wait_send()

    def back(h, p, yy):
        return remote(
            rsend.at[h, p], rrecv.at[h, yy], r_send.at[h, p], r_recv.at[h, yy], at_y(p)
        )

    def step(it, carry):
        def z_copy(c, t, src):
            return remote(
                zsend.at[c, t], zrecv.at[it, c, src], z_send.at[c, t], z_recv.at[it, c, src], at_z(t)
            )

        def rel_copy(c):
            return remote(
                zsend.at[c, far], zrel.at[it, c], z_send.at[c, far], rel_recv.at[it, c], at_z(near)
            )

        def hand_on(c):
            mine = wfull.at[it, c, far]
            return remote(mine, mine, w_send.at[c, z], w_recv.at[it, c, far], at_z(near))

        def where(cond, run):
            if line:
                pl.when(cond)(run)
            else:
                run()

        def w_copy(c, t, src):
            mine = wfull.at[it, c, src]
            return remote(mine, mine, w_send.at[c, t], w_recv.at[it, c, src], at_z(t))

        def predict(c):
            h, r = c // B, rows_y[c % B]
            if c % B == 0:
                @pl.when(it == 0)
                def _():
                    for p in y_peers:
                        d_y(h, p, p).wait_recv()

                scaled[...] = (
                    d_full[pl.ds(h * W, W)].astype(jnp.float32) * mu_ref[...]
                ).astype(jnp.bfloat16)
            rows = jnp.concatenate([s_full[a * B + r] for a in range(A)], axis=0)
            part = lax.dot_general(
                rows, scaled[...], (((1,), (1,)), ((), ())), preferred_element_type=jnp.float32
            ).reshape(A, R, W)
            zsend[c] = part.astype(jnp.bfloat16)
            for t in z_peers:
                where(t != far, lambda: z_copy(c, t, z).start())
            if line:
                @pl.when(inner == 0)
                def _():
                    rel_copy(c).start()
            own[c] = part

        def relay(c):
            if line:
                @pl.when(inner == 1)
                def _():
                    rel_copy(c).wait_recv()
                    zsend[c, far] = (own[c, far] + zrel[it, c].astype(jnp.float32)).astype(jnp.bfloat16)
                    z_copy(c, far, z).start()

        def forward(c):
            if line:
                @pl.when(inner == 1)
                def _():
                    w_copy(c, far, far).wait_recv()
                    hand_on(c).start()

        def over_z(c):
            h, k = c // B, c % B
            r = rows_y[k]
            if h == 0 and k > 0:
                @pl.when(it == 0)
                def _():
                    for copy in pairs(r, r)[1:]:
                        copy.wait_recv()

            for t in z_peers:
                def add():
                    z_copy(c, t, t).wait_recv()
                    own[c, z] = own[c, z] + zrecv[it, c, t].astype(jnp.float32)

                where(jnp.logical_or(inner == 1, t != far), add)
            total = own[c, z]
            here = pl.ds(h * W, W)
            code = code_ref[r, :, here].astype(jnp.float32)
            weight = jnp.where(code > 0.0, 1.0 / jnp.maximum(code, 1.0), 0.0)
            weighted = weight * (total * pred_scale - meas_ref[r, :, here])
            wfull[it, c, z] = weighted.astype(jnp.bfloat16)
            for t in z_peers:
                where(jnp.logical_or(inner == 1, t != far), lambda: w_copy(c, t, z).start())
            rsend[h, r] = weighted
            if k > 0:
                @pl.when(it == ITERS - 1)
                def _():
                    back(h, r, y).start()

        def gradient(c, total):
            h, r = c // B, rows_y[c % B]
            for t in z_peers:
                where(jnp.logical_or(inner == 0, t != far), lambda: w_copy(c, t, t).wait_recv())
            d = d_full[pl.ds(h * W, W)]

            def rows(i, total):
                w = wfull[it, c, pl.ds(2 * i, 2)].reshape(2 * R, W)
                s = jnp.concatenate([s_full[(2 * i + k) * B + r] for k in range(2)], axis=0)
                inner = jnp.dot(w, d, preferred_element_type=jnp.float32) * s.astype(jnp.float32)
                return total + jnp.sum(inner.reshape(2 * R // 8, 8, B * X), axis=0)

            return lax.fori_loop(0, A // 2, rows, total)

        total = jnp.zeros((8, B * X), jnp.float32)
        for c in range(min(2, C)):
            predict(c)
        relay(0)
        for slot in range(C + 2):
            if slot + 2 < C:
                predict(slot + 2)
            if slot + 1 < C:
                relay(slot + 1)
            if 0 < slot <= C:
                forward(slot - 1)
            if slot < C:
                over_z(slot)
            if slot > 1:
                total = gradient(slot - 2, total)

        def g_copy(p, j, sp, sj):
            mine = gbuf.at[it, sp * NO + sj]
            return remote(
                mine, mine, g_send.at[p * NO + j], g_recv.at[it, sp * NO + sj],
                {"vox": z * B + p, "opt": j},
            )

        gbuf[it, y * NO + opt] = jnp.sum(total, axis=0, keepdims=True)
        for p, j in group:
            g_copy(p, j, y, opt).start()
        for c in range(C):
            for t in z_peers:
                z_copy(c, t, z).wait_send()
                where(jnp.logical_or(inner == 1, t != far), lambda: w_copy(c, t, z).wait_send())
            if line:
                @pl.when(inner == 1)
                def _():
                    hand_on(c).wait_send()
        for p, j in group:
            g_copy(p, j, p, j).wait_recv()
        grad = gbuf[it, 0]
        for j in range(1, B * NO):
            grad = grad + gbuf[it, j]
        mu_ref[...] = jnp.maximum(mu_ref[...] - 2.0 * (grad * grad_scale), 0.0)
        for p, j in group:
            g_copy(p, j, y, opt).wait_send()
        return carry

    lax.fori_loop(0, ITERS, step, 0)
    mu_out[...] = mu_ref[:, half(y)]
    for h in range(NH):
        res_ref[:, pl.ds(pl.multiple_of(y * H + h * W, W), W)] = rsend[h, y]
        for p in y_peers:
            back(h, p, p).wait_recv()
            res_ref[:, pl.ds(pl.multiple_of(p * H + h * W, W), W)] = rrecv[h, p]
            back(h, p, y).wait_send()
            d_y(h, p, y).wait_send()
    for p in y_peers:
        for copy in pairs(p, y):
            copy.wait_send()


def local(source_fields, detector_fields, measured, valid_pair, weight_class, absorption):
    NV, NO = lax.axis_size("vox"), lax.axis_size("opt")
    R, DL = measured.shape
    X = absorption.shape[0]
    q = source_fields.shape[0] // R
    B = 2 if DL % 256 == 0 and NV % 4 == 0 else 1
    A = NV // B
    H = DL // B
    W = min(H, 256)
    NH = H // W
    C = NH * B
    pred_scale = float(np.float32(1.0) / np.sqrt(np.float32(X * NV)))
    grad_scale = float(np.sqrt(np.float32(X * NV)) / np.float32(R * NV * DL * NO))
    bf, f32 = jnp.bfloat16, jnp.float32
    dma = pltpu.SemaphoreType.DMA
    vmem = pl.BlockSpec(memory_space=pltpu.VMEM)
    mu, weighted = pl.pallas_call(
        functools.partial(kernel, A, B, NO, W, pred_scale, grad_scale),
        out_shape=(
            jax.ShapeDtypeStruct((1, X), f32),
            jax.ShapeDtypeStruct((R, DL), f32),
        ),
        in_specs=[pl.BlockSpec(memory_space=pl.ANY)] * 5 + [vmem],
        out_specs=(vmem, vmem),
        scratch_shapes=[
            pltpu.VMEM((A * B, R, B * X), bf),
            pltpu.VMEM((H, B * X), bf),
            pltpu.VMEM((B, R, H), f32),
            pltpu.VMEM((R, DL), jnp.int32),
            pltpu.VMEM((R, DL), jnp.int32),
            pltpu.VMEM((R, DL), bf),
            pltpu.VMEM((B, R, H), bf),
            pltpu.VMEM((1, B * X), f32),
            pltpu.VMEM((W, B * X), bf),
            pltpu.VMEM((C, A, R, W), f32),
            pltpu.VMEM((C, A, R, W), bf),
            pltpu.VMEM((ITERS, C, A, R, W), bf),
            pltpu.VMEM((ITERS, C, R, W), bf),
            pltpu.VMEM((ITERS, C, A, R, W), bf),
            pltpu.VMEM((NH, B, R, W), f32),
            pltpu.VMEM((NH, B, R, W), f32),
            pltpu.VMEM((ITERS, B * NO, 1, B * X), f32),
            dma((B,)), dma((B,)),
            dma((NO // 2, B)), dma((NO // 2, B)),
            dma((NO // 2, B)), dma((NO // 2, B)),
            dma((NH, B)), dma((NH, B)),
            dma((3, B)), dma((3, B)),
            dma((NH, B)), dma((NH, B)),
            dma((C, A)), dma((ITERS, C, A)), dma((ITERS, C)),
            dma((C, A)), dma((ITERS, C, A)),
            dma((B * NO,)), dma((ITERS, B * NO)),
            dma((4 + NH,)),
        ],
        compiler_params=pltpu.CompilerParams(
            collective_id=0, has_side_effects=True, vmem_limit_bytes=52 * 1024 * 1024
        ),
    )(
        source_fields.reshape(q, R, X), detector_fields, measured, valid_pair, weight_class,
        absorption.reshape(1, X),
    )
    return mu.reshape(X), weighted


def solution(mesh):
    placed = (
        P("opt", "vox"),
        P("opt", "vox"),
        P("vox", "opt"),
        P("vox", "opt"),
        P("vox", "opt"),
        P("vox"),
    )
    return jax.shard_map(
        local, mesh=mesh, in_specs=placed, out_specs=(P("vox"), P("vox", "opt")), check_vma=False
    )
```

```python
import functools

import jax
import jax.numpy as jnp
import numpy as np
from jax import lax
from jax.experimental import pallas as pl
from jax.experimental.pallas import tpu as pltpu
from jax.sharding import PartitionSpec as P

ITERS = 2
MESH = pl.DeviceIdType.MESH


def kernel(
    A, B, NO, W, pred_scale, grad_scale,
    s_in, d_in, meas_in, valid_in, class_in, mu_in,
    mu_out, res_ref,
    s_full, d_full, meas_ref, valid_ref, class_ref, codes, code_ref, mu_ref, scaled,
    own, zsend, zrecv, zrel, wfull, rsend, rrecv, gbuf,
    sy_send, sy_recv, sx_send, sx_recv, sm_send, sm_recv, d_send, d_recv,
    p_send, p_recv, r_send, r_recv, z_send, z_recv, rel_send, rel_recv, h_send, w_send, w_recv, g_send, g_recv, in_sem,
):
    q, R, X = s_in.shape
    H = d_in.shape[0] // B
    NH = H // W
    C = NH * B
    vox = lax.axis_index("vox")
    opt = lax.axis_index("opt")
    z, y = vox // B, lax.rem(vox, B)
    chip, core = opt // 2, lax.rem(opt, 2)
    NC = NO // 2
    mate = chip * 2 + 1 - core
    rows_y = [lax.rem(y + k, B) for k in range(B)]
    y_peers = rows_y[1:]
    z_peers = [lax.rem(z + k, A) for k in range(1, A)]
    line = A == 4
    inner = lax.rem((z + 1) // 2, 2)
    near = inner * 3 * (z - 1) + (1 - inner) * (1 + z // 3)
    across = 2 - z // 2
    base = 2 * (1 - z // 2)
    z_direct = [near] if line else z_peers
    z_adds = [near, across] if line else z_peers
    c_peers = [lax.rem(chip + k, NC) for k in range(1, NC)]
    group = [
        (lax.rem(y + k, B), lax.rem(opt + j, NO)) for k in range(B) for j in range(NO) if k + j > 0
    ]

    def remote(src, dst, send, recv, where):
        return pltpu.make_async_remote_copy(
            src_ref=src, dst_ref=dst, send_sem=send, recv_sem=recv,
            device_id=where, device_id_type=MESH,
        )

    def half(yy):
        return pl.ds(pl.multiple_of(yy * X, X), X)

    def cols(yy):
        return pl.ds(pl.multiple_of(yy * H, H), H)

    def at_y(p):
        return {"vox": z * B + p}

    def at_z(t):
        return {"vox": t * B + y}

    def block(j, yy):
        return s_full.at[pl.ds(j * q, q), :, half(yy)]

    def d_block(h, yy):
        return d_full.at[pl.ds(h * W, W), half(yy)]

    def d_rows(h, yy):
        return d_in.at[pl.ds(pl.multiple_of(yy * H + h * W, W), W)]

    loads = [
        pltpu.make_async_copy(valid_in, valid_ref, in_sem.at[0]),
        pltpu.make_async_copy(class_in, class_ref, in_sem.at[1]),
        pltpu.make_async_copy(s_in, block(opt, y), in_sem.at[2]),
        pltpu.make_async_copy(meas_in.at[:, cols(y)], meas_ref.at[y], in_sem.at[3]),
    ] + [
        pltpu.make_async_copy(d_rows(h, y), d_block(h, y), in_sem.at[4 + h]) for h in range(NH)
    ]
    for load in loads:
        load.start()

    barrier = pltpu.get_barrier_semaphore()
    for t in z_peers:
        pl.semaphore_signal(barrier, inc=1, device_id=at_z(t), device_id_type=MESH)
    for p, j in group:
        pl.semaphore_signal(
            barrier, inc=1, device_id={"vox": z * B + p, "opt": j}, device_id_type=MESH
        )
    pl.semaphore_wait(barrier, A - 1 + B * NO - 1)

    def s_y(p, yy):
        return remote(s_in, block(opt, yy), sy_send.at[p], sy_recv.at[yy], at_y(p))

    def s_x(p, j, yy):
        return remote(
            block(j, yy), block(j, yy), sx_send.at[p, yy], sx_recv.at[j // 2, yy],
            {"opt": p * 2 + core},
        )

    def s_x_own(p):
        return remote(
            s_in, block(opt, y), sx_send.at[p, y], sx_recv.at[chip, y], {"opt": p * 2 + core}
        )

    def s_m(p, cc, yy):
        mine = block(p * 2 + cc, yy)
        return remote(mine, mine, sm_send.at[p, yy], sm_recv.at[p, yy], {"opt": mate})

    def s_m_own():
        return remote(s_in, block(opt, y), sm_send.at[chip, y], sm_recv.at[chip, y], {"opt": mate})

    def d_y(h, p, yy):
        return remote(d_rows(h, p), d_block(h, yy), d_send.at[h, p], d_recv.at[h, yy], at_y(p))

    def pairs(p, yy):
        return [
            remote(mu_in, mu_ref.at[:, half(yy)], p_send.at[0, p], p_recv.at[0, yy], at_y(p)),
            remote(
                meas_in.at[:, cols(p)], meas_ref.at[yy], p_send.at[1, p], p_recv.at[1, yy], at_y(p)
            ),
            remote(
                codes.at[:, cols(p)], code_ref.at[yy], p_send.at[2, p], p_recv.at[2, yy], at_y(p)
            ),
        ]

    for p in y_peers:
        s_y(p, y).start()
    for p in c_peers:
        s_x_own(p).start()
    s_m_own().start()
    for p in y_peers:
        pairs(p, y)[0].start()
    for load in loads:
        load.wait()
    mu_ref[:, half(y)] = mu_in[...]
    codes[...] = (valid_ref[...] * (1 + class_ref[...])).astype(jnp.float32).astype(jnp.bfloat16)
    code_ref[y] = codes[:, cols(y)]
    for p in y_peers:
        s_y(p, p).wait_recv()
        d_y(0, p, y).start()
        for pp in c_peers:
            s_x(pp, opt, p).start()
        s_m(chip, core, p).start()
    for yy in rows_y:
        for p in c_peers:
            s_x(p, p * 2 + core, yy).wait_recv()
            s_m(p, core, yy).start()
    for p in y_peers:
        for copy in pairs(p, y)[1:]:
            copy.start()
        for h in range(1, NH):
            d_y(h, p, y).start()
    for yy in rows_y:
        for p in range(NC):
            s_m(p, 1 - core, yy).wait_recv()
    for p in y_peers:
        pairs(p, p)[0].wait_recv()
        s_y(p, y).wait_send()
    for p in c_peers:
        s_x_own(p).wait_send()
        for yy in y_peers:
            s_x(p, opt, yy).wait_send()
    for p in range(NC):
        for yy in rows_y:
            s_m(p, core, yy).wait_send()

    def back(h, p, yy):
        return remote(
            rsend.at[h, p], rrecv.at[h, yy], r_send.at[h, p], r_recv.at[h, yy], at_y(p)
        )

    def step(it, carry):
        def z_copy(c, t, src):
            return remote(
                zsend.at[c, t], zrecv.at[it, c, src], z_send.at[c, t], z_recv.at[it, c, src], at_z(t)
            )

        def rel_copy(c):
            return remote(
                zsend.at[c, pl.ds(base, 2)], zrel.at[it, c], rel_send.at[c], rel_recv.at[it, c],
                at_z(near),
            )

        def hand_on(c, src):
            mine = wfull.at[it, c, src]
            return remote(mine, mine, h_send.at[c, src], w_recv.at[it, c, src], at_z(near))

        def w_copy(c, t, src):
            mine = wfull.at[it, c, src]
            return remote(mine, mine, w_send.at[c, t], w_recv.at[it, c, src], at_z(t))

        def predict(c):
            h, r = c // B, rows_y[c % B]
            if c % B == 0:
                @pl.when(it == 0)
                def _():
                    for p in y_peers:
                        d_y(h, p, p).wait_recv()

                scaled[...] = (
                    d_full[pl.ds(h * W, W)].astype(jnp.float32) * mu_ref[...]
                ).astype(jnp.bfloat16)
            rows = jnp.concatenate([s_full[a * B + r] for a in range(A)], axis=0)
            part = lax.dot_general(
                rows, scaled[...], (((1,), (1,)), ((), ())), preferred_element_type=jnp.float32
            ).reshape(A, R, W)
            zsend[c] = part.astype(jnp.bfloat16)
            for t in z_direct:
                z_copy(c, t, z).start()
            if line:
                @pl.when(inner == 0)
                def _():
                    rel_copy(c).start()
            own[c] = part

        def relay(c):
            if line:
                @pl.when(inner == 1)
                def _():
                    rel_copy(c).wait_recv()
                    both = pl.ds(base, 2)
                    total = own[c, both] + zrel[it, c].astype(jnp.float32)
                    zsend[c, both] = total.astype(jnp.bfloat16)
                    for k in range(2):
                        z_copy(c, base + k, z).start()

        def forward(c):
            if line:
                @pl.when(inner == 1)
                def _():
                    for k in range(2):
                        w_copy(c, base + k, base + k).wait_recv()
                        hand_on(c, base + k).start()

        def over_z(c):
            h, k = c // B, c % B
            r = rows_y[k]
            if h == 0 and k > 0:
                @pl.when(it == 0)
                def _():
                    for copy in pairs(r, r)[1:]:
                        copy.wait_recv()

            total = own[c, z]
            for t in z_adds:
                z_copy(c, t, t).wait_recv()
                total = total + zrecv[it, c, t].astype(jnp.float32)
            here = pl.ds(h * W, W)
            code = code_ref[r, :, here].astype(jnp.float32)
            weight = jnp.where(code > 0.0, 1.0 / jnp.maximum(code, 1.0), 0.0)
            weighted = weight * (total * pred_scale - meas_ref[r, :, here])
            wfull[it, c, z] = weighted.astype(jnp.bfloat16)
            for t in z_adds:
                w_copy(c, t, z).start()
            rsend[h, r] = weighted
            if k > 0:
                @pl.when(it == ITERS - 1)
                def _():
                    back(h, r, y).start()

        def gradient(c, total):
            h, r = c // B, rows_y[c % B]
            for t in z_direct:
                w_copy(c, t, t).wait_recv()
            if line:
                @pl.when(inner == 0)
                def _():
                    for k in range(2):
                        w_copy(c, base + k, base + k).wait_recv()
            d = d_full[pl.ds(h * W, W)]

            def rows(i, total):
                w = wfull[it, c, pl.ds(2 * i, 2)].reshape(2 * R, W)
                s = jnp.concatenate([s_full[(2 * i + k) * B + r] for k in range(2)], axis=0)
                inner = jnp.dot(w, d, preferred_element_type=jnp.float32) * s.astype(jnp.float32)
                return total + jnp.sum(inner.reshape(2 * R // 8, 8, B * X), axis=0)

            return lax.fori_loop(0, A // 2, rows, total)

        total = jnp.zeros((8, B * X), jnp.float32)
        for c in range(min(2, C)):
            predict(c)
        relay(0)
        for slot in range(C + 2):
            if slot + 2 < C:
                predict(slot + 2)
            if slot + 1 < C:
                relay(slot + 1)
            if 0 < slot <= C:
                forward(slot - 1)
            if slot < C:
                over_z(slot)
            if slot > 1:
                total = gradient(slot - 2, total)

        def g_copy(p, j, sp, sj):
            mine = gbuf.at[it, sp * NO + sj]
            return remote(
                mine, mine, g_send.at[p * NO + j], g_recv.at[it, sp * NO + sj],
                {"vox": z * B + p, "opt": j},
            )

        gbuf[it, y * NO + opt] = jnp.sum(total, axis=0, keepdims=True)
        for p, j in group:
            g_copy(p, j, y, opt).start()
        for c in range(C):
            for t in z_direct:
                z_copy(c, t, z).wait_send()
            for t in z_adds:
                w_copy(c, t, z).wait_send()
            if line:
                @pl.when(inner == 1)
                def _():
                    for k in range(2):
                        z_copy(c, base + k, z).wait_send()
                        hand_on(c, base + k).wait_send()

                @pl.when(inner == 0)
                def _():
                    rel_copy(c).wait_send()
        for p, j in group:
            g_copy(p, j, p, j).wait_recv()
        grad = gbuf[it, 0]
        for j in range(1, B * NO):
            grad = grad + gbuf[it, j]
        mu_ref[...] = jnp.maximum(mu_ref[...] - 2.0 * (grad * grad_scale), 0.0)
        for p, j in group:
            g_copy(p, j, y, opt).wait_send()
        return carry

    lax.fori_loop(0, ITERS, step, 0)
    mu_out[...] = mu_ref[:, half(y)]
    for h in range(NH):
        res_ref[:, pl.ds(pl.multiple_of(y * H + h * W, W), W)] = rsend[h, y]
        for p in y_peers:
            back(h, p, p).wait_recv()
            res_ref[:, pl.ds(pl.multiple_of(p * H + h * W, W), W)] = rrecv[h, p]
            back(h, p, y).wait_send()
            d_y(h, p, y).wait_send()
    for p in y_peers:
        for copy in pairs(p, y):
            copy.wait_send()


def local(source_fields, detector_fields, measured, valid_pair, weight_class, absorption):
    NV, NO = lax.axis_size("vox"), lax.axis_size("opt")
    R, DL = measured.shape
    X = absorption.shape[0]
    q = source_fields.shape[0] // R
    B = 2 if DL % 256 == 0 and NV % 4 == 0 else 1
    A = NV // B
    H = DL // B
    W = min(H, 256)
    NH = H // W
    C = NH * B
    pred_scale = float(np.float32(1.0) / np.sqrt(np.float32(X * NV)))
    grad_scale = float(np.sqrt(np.float32(X * NV)) / np.float32(R * NV * DL * NO))
    bf, f32 = jnp.bfloat16, jnp.float32
    dma = pltpu.SemaphoreType.DMA
    vmem = pl.BlockSpec(memory_space=pltpu.VMEM)
    mu, weighted = pl.pallas_call(
        functools.partial(kernel, A, B, NO, W, pred_scale, grad_scale),
        out_shape=(
            jax.ShapeDtypeStruct((1, X), f32),
            jax.ShapeDtypeStruct((R, DL), f32),
        ),
        in_specs=[pl.BlockSpec(memory_space=pl.ANY)] * 5 + [vmem],
        out_specs=(vmem, vmem),
        scratch_shapes=[
            pltpu.VMEM((A * B, R, B * X), bf),
            pltpu.VMEM((H, B * X), bf),
            pltpu.VMEM((B, R, H), f32),
            pltpu.VMEM((R, DL), jnp.int32),
            pltpu.VMEM((R, DL), jnp.int32),
            pltpu.VMEM((R, DL), bf),
            pltpu.VMEM((B, R, H), bf),
            pltpu.VMEM((1, B * X), f32),
            pltpu.VMEM((W, B * X), bf),
            pltpu.VMEM((C, A, R, W), f32),
            pltpu.VMEM((C, A, R, W), bf),
            pltpu.VMEM((ITERS, C, A, R, W), bf),
            pltpu.VMEM((ITERS, C, 2, R, W), bf),
            pltpu.VMEM((ITERS, C, A, R, W), bf),
            pltpu.VMEM((NH, B, R, W), f32),
            pltpu.VMEM((NH, B, R, W), f32),
            pltpu.VMEM((ITERS, B * NO, 1, B * X), f32),
            dma((B,)), dma((B,)),
            dma((NO // 2, B)), dma((NO // 2, B)),
            dma((NO // 2, B)), dma((NO // 2, B)),
            dma((NH, B)), dma((NH, B)),
            dma((3, B)), dma((3, B)),
            dma((NH, B)), dma((NH, B)),
            dma((C, A)), dma((ITERS, C, A)), dma((C,)), dma((ITERS, C)), dma((C, A)),
            dma((C, A)), dma((ITERS, C, A)),
            dma((B * NO,)), dma((ITERS, B * NO)),
            dma((4 + NH,)),
        ],
        compiler_params=pltpu.CompilerParams(
            collective_id=0, has_side_effects=True, vmem_limit_bytes=52 * 1024 * 1024
        ),
    )(
        source_fields.reshape(q, R, X), detector_fields, measured, valid_pair, weight_class,
        absorption.reshape(1, X),
    )
    return mu.reshape(X), weighted


def solution(mesh):
    placed = (
        P("opt", "vox"),
        P("opt", "vox"),
        P("vox", "opt"),
        P("vox", "opt"),
        P("vox", "opt"),
        P("vox"),
    )
    return jax.shard_map(
        local, mesh=mesh, in_specs=placed, out_specs=(P("vox"), P("vox", "opt")), check_vma=False
    )
```

```python
import functools

import jax
import jax.numpy as jnp
import numpy as np
from jax import lax
from jax.experimental import pallas as pl
from jax.experimental.pallas import tpu as pltpu
from jax.sharding import PartitionSpec as P

ITERS = 2
MESH = pl.DeviceIdType.MESH


def kernel(
    A, B, NO, W, pred_scale, grad_scale,
    s_in, d_in, meas_in, valid_in, class_in, mu_in,
    mu_out, res_ref,
    s_full, d_full, meas_ref, valid_ref, class_ref, codes, code_ref, mu_ref, scaled,
    own, zsend, zrecv, zrel, wfull, rsend, rrecv, gbuf,
    sy_send, sy_recv, sx_send, sx_recv, sm_send, sm_recv, d_send, d_recv,
    p_send, p_recv, r_send, r_recv, z_send, z_recv, rel_send, rel_recv, h_send, w_send, w_recv, g_send, g_recv, in_sem,
):
    q, R, X = s_in.shape
    H = d_in.shape[0] // B
    NH = H // W
    F = 2
    C = NH * B * F
    Q = R // F
    vox = lax.axis_index("vox")
    opt = lax.axis_index("opt")
    z, y = vox // B, lax.rem(vox, B)
    chip, core = opt // 2, lax.rem(opt, 2)
    NC = NO // 2
    mate = chip * 2 + 1 - core
    rows_y = [lax.rem(y + k, B) for k in range(B)]
    y_peers = rows_y[1:]
    z_peers = [lax.rem(z + k, A) for k in range(1, A)]
    line = A == 4
    inner = lax.rem((z + 1) // 2, 2)
    near = inner * 3 * (z - 1) + (1 - inner) * (1 + z // 3)
    across = 2 - z // 2
    base = 2 * (1 - z // 2)
    z_direct = [near] if line else z_peers
    z_adds = [near, across] if line else z_peers
    c_peers = [lax.rem(chip + k, NC) for k in range(1, NC)]
    group = [
        (lax.rem(y + k, B), lax.rem(opt + j, NO)) for k in range(B) for j in range(NO) if k + j > 0
    ]

    def remote(src, dst, send, recv, where):
        return pltpu.make_async_remote_copy(
            src_ref=src, dst_ref=dst, send_sem=send, recv_sem=recv,
            device_id=where, device_id_type=MESH,
        )

    def half(yy):
        return pl.ds(pl.multiple_of(yy * X, X), X)

    def cols(yy):
        return pl.ds(pl.multiple_of(yy * H, H), H)

    def at_y(p):
        return {"vox": z * B + p}

    def at_z(t):
        return {"vox": t * B + y}

    def block(j, yy):
        return s_full.at[pl.ds(j * q, q), :, half(yy)]

    def d_block(h, yy):
        return d_full.at[pl.ds(h * W, W), half(yy)]

    def d_rows(h, yy):
        return d_in.at[pl.ds(pl.multiple_of(yy * H + h * W, W), W)]

    loads = [
        pltpu.make_async_copy(valid_in, valid_ref, in_sem.at[0]),
        pltpu.make_async_copy(class_in, class_ref, in_sem.at[1]),
        pltpu.make_async_copy(s_in, block(opt, y), in_sem.at[2]),
        pltpu.make_async_copy(meas_in.at[:, cols(y)], meas_ref.at[y], in_sem.at[3]),
    ] + [
        pltpu.make_async_copy(d_rows(h, y), d_block(h, y), in_sem.at[4 + h]) for h in range(NH)
    ]
    for load in loads:
        load.start()

    barrier = pltpu.get_barrier_semaphore()
    for t in z_peers:
        pl.semaphore_signal(barrier, inc=1, device_id=at_z(t), device_id_type=MESH)
    for p, j in group:
        pl.semaphore_signal(
            barrier, inc=1, device_id={"vox": z * B + p, "opt": j}, device_id_type=MESH
        )
    pl.semaphore_wait(barrier, A - 1 + B * NO - 1)

    def s_y(p, yy):
        return remote(s_in, block(opt, yy), sy_send.at[p], sy_recv.at[yy], at_y(p))

    def s_x(p, j, yy):
        return remote(
            block(j, yy), block(j, yy), sx_send.at[p, yy], sx_recv.at[j // 2, yy],
            {"opt": p * 2 + core},
        )

    def s_x_own(p):
        return remote(
            s_in, block(opt, y), sx_send.at[p, y], sx_recv.at[chip, y], {"opt": p * 2 + core}
        )

    def s_m(p, cc, yy):
        mine = block(p * 2 + cc, yy)
        return remote(mine, mine, sm_send.at[p, yy], sm_recv.at[p, yy], {"opt": mate})

    def s_m_own():
        return remote(s_in, block(opt, y), sm_send.at[chip, y], sm_recv.at[chip, y], {"opt": mate})

    def d_y(h, p, yy):
        return remote(d_rows(h, p), d_block(h, yy), d_send.at[h, p], d_recv.at[h, yy], at_y(p))

    def pairs(p, yy):
        return [
            remote(mu_in, mu_ref.at[:, half(yy)], p_send.at[0, p], p_recv.at[0, yy], at_y(p)),
            remote(
                meas_in.at[:, cols(p)], meas_ref.at[yy], p_send.at[1, p], p_recv.at[1, yy], at_y(p)
            ),
            remote(
                codes.at[:, cols(p)], code_ref.at[yy], p_send.at[2, p], p_recv.at[2, yy], at_y(p)
            ),
        ]

    for p in y_peers:
        s_y(p, y).start()
    for p in c_peers:
        s_x_own(p).start()
    s_m_own().start()
    for p in y_peers:
        pairs(p, y)[0].start()
    for load in loads:
        load.wait()
    mu_ref[:, half(y)] = mu_in[...]
    codes[...] = (valid_ref[...] * (1 + class_ref[...])).astype(jnp.float32).astype(jnp.bfloat16)
    code_ref[y] = codes[:, cols(y)]
    for p in y_peers:
        s_y(p, p).wait_recv()
        d_y(0, p, y).start()
        for pp in c_peers:
            s_x(pp, opt, p).start()
        s_m(chip, core, p).start()
    for yy in rows_y:
        for p in c_peers:
            s_x(p, p * 2 + core, yy).wait_recv()
            s_m(p, core, yy).start()
    for p in y_peers:
        for copy in pairs(p, y)[1:]:
            copy.start()
        for h in range(1, NH):
            d_y(h, p, y).start()
    for yy in rows_y:
        for p in range(NC):
            s_m(p, 1 - core, yy).wait_recv()
    for p in y_peers:
        pairs(p, p)[0].wait_recv()
        s_y(p, y).wait_send()
    for p in c_peers:
        s_x_own(p).wait_send()
        for yy in y_peers:
            s_x(p, opt, yy).wait_send()
    for p in range(NC):
        for yy in rows_y:
            s_m(p, core, yy).wait_send()

    def back(h, p, yy):
        return remote(
            rsend.at[h, p], rrecv.at[h, yy], r_send.at[h, p], r_recv.at[h, yy], at_y(p)
        )

    def step(it, carry):
        def z_copy(c, t, src):
            return remote(
                zsend.at[c, t], zrecv.at[it, c, src], z_send.at[c, t], z_recv.at[it, c, src], at_z(t)
            )

        def rel_copy(c):
            return remote(
                zsend.at[c, pl.ds(base, 2)], zrel.at[it, c], rel_send.at[c], rel_recv.at[it, c],
                at_z(near),
            )

        def hand_on(c, src):
            mine = wfull.at[it, c, src]
            return remote(mine, mine, h_send.at[c, src], w_recv.at[it, c, src], at_z(near))

        def w_copy(c, t, src):
            mine = wfull.at[it, c, src]
            return remote(mine, mine, w_send.at[c, t], w_recv.at[it, c, src], at_z(t))

        def rows_of(c):
            r, f = rows_y[c // F % B], c % F
            return jnp.concatenate(
                [s_full[a * B + r, pl.ds(f * Q, Q)] for a in range(A)], axis=0
            )

        def predict(c):
            h, r = c // (B * F), rows_y[c // F % B]
            if c % (B * F) == 0:
                @pl.when(it == 0)
                def _():
                    for p in y_peers:
                        d_y(h, p, p).wait_recv()

                scaled[...] = (
                    d_full[pl.ds(h * W, W)].astype(jnp.float32) * mu_ref[...]
                ).astype(jnp.bfloat16)
            rows = rows_of(c)
            part = lax.dot_general(
                rows, scaled[...], (((1,), (1,)), ((), ())), preferred_element_type=jnp.float32
            ).reshape(A, Q, W)
            zsend[c] = part.astype(jnp.bfloat16)
            for t in z_direct:
                z_copy(c, t, z).start()
            if line:
                @pl.when(inner == 0)
                def _():
                    rel_copy(c).start()
            own[c] = part

        def relay(c):
            if line:
                @pl.when(inner == 1)
                def _():
                    rel_copy(c).wait_recv()
                    both = pl.ds(base, 2)
                    total = own[c, both] + zrel[it, c].astype(jnp.float32)
                    zsend[c, both] = total.astype(jnp.bfloat16)
                    for k in range(2):
                        z_copy(c, base + k, z).start()

        def forward(c):
            if line:
                @pl.when(inner == 1)
                def _():
                    for k in range(2):
                        w_copy(c, base + k, base + k).wait_recv()
                        hand_on(c, base + k).start()

        def over_z(c):
            h, k, f = c // (B * F), c // F % B, c % F
            r = rows_y[k]
            if h == 0 and k > 0 and f == 0:
                @pl.when(it == 0)
                def _():
                    for copy in pairs(r, r)[1:]:
                        copy.wait_recv()

            total = own[c, z]
            for t in z_adds:
                z_copy(c, t, t).wait_recv()
                total = total + zrecv[it, c, t].astype(jnp.float32)
            here, part = pl.ds(h * W, W), pl.ds(f * Q, Q)
            code = code_ref[r, part, here].astype(jnp.float32)
            weight = jnp.where(code > 0.0, 1.0 / jnp.maximum(code, 1.0), 0.0)
            weighted = weight * (total * pred_scale - meas_ref[r, part, here])
            wfull[it, c, z] = weighted.astype(jnp.bfloat16)
            for t in z_adds:
                w_copy(c, t, z).start()
            rsend[h, r, part] = weighted
            if k > 0 and f == F - 1:
                @pl.when(it == ITERS - 1)
                def _():
                    back(h, r, y).start()

        def gradient(c, total):
            h = c // (B * F)
            for t in z_direct:
                w_copy(c, t, t).wait_recv()
            if line:
                @pl.when(inner == 0)
                def _():
                    for k in range(2):
                        w_copy(c, base + k, base + k).wait_recv()
            w = wfull[it, c].reshape(A * Q, W)
            summed = jnp.dot(w, d_full[pl.ds(h * W, W)], preferred_element_type=jnp.float32)
            summed = summed * rows_of(c).astype(jnp.float32)
            return total + jnp.sum(summed.reshape(A * Q // 8, 8, B * X), axis=0)

        total = jnp.zeros((8, B * X), jnp.float32)
        for c in range(min(2, C)):
            predict(c)
        relay(0)
        for slot in range(C + 3):
            if slot + 2 < C:
                predict(slot + 2)
            if slot + 1 < C:
                relay(slot + 1)
            if slot < C:
                over_z(slot)
            if 0 < slot <= C:
                forward(slot - 1)
            if slot > 2:
                total = gradient(slot - 3, total)

        def g_copy(p, j, sp, sj):
            mine = gbuf.at[it, sp * NO + sj]
            return remote(
                mine, mine, g_send.at[p * NO + j], g_recv.at[it, sp * NO + sj],
                {"vox": z * B + p, "opt": j},
            )

        gbuf[it, y * NO + opt] = jnp.sum(total, axis=0, keepdims=True)
        for p, j in group:
            g_copy(p, j, y, opt).start()
        for c in range(C):
            for t in z_direct:
                z_copy(c, t, z).wait_send()
            for t in z_adds:
                w_copy(c, t, z).wait_send()
            if line:
                @pl.when(inner == 1)
                def _():
                    for k in range(2):
                        z_copy(c, base + k, z).wait_send()
                        hand_on(c, base + k).wait_send()

                @pl.when(inner == 0)
                def _():
                    rel_copy(c).wait_send()
        for p, j in group:
            g_copy(p, j, p, j).wait_recv()
        grad = gbuf[it, 0]
        for j in range(1, B * NO):
            grad = grad + gbuf[it, j]
        mu_ref[...] = jnp.maximum(mu_ref[...] - 2.0 * (grad * grad_scale), 0.0)
        for p, j in group:
            g_copy(p, j, y, opt).wait_send()
        return carry

    lax.fori_loop(0, ITERS, step, 0)
    mu_out[...] = mu_ref[:, half(y)]
    for h in range(NH):
        res_ref[:, pl.ds(pl.multiple_of(y * H + h * W, W), W)] = rsend[h, y]
        for p in y_peers:
            back(h, p, p).wait_recv()
            res_ref[:, pl.ds(pl.multiple_of(p * H + h * W, W), W)] = rrecv[h, p]
            back(h, p, y).wait_send()
            d_y(h, p, y).wait_send()
    for p in y_peers:
        for copy in pairs(p, y):
            copy.wait_send()


def local(source_fields, detector_fields, measured, valid_pair, weight_class, absorption):
    NV, NO = lax.axis_size("vox"), lax.axis_size("opt")
    R, DL = measured.shape
    X = absorption.shape[0]
    q = source_fields.shape[0] // R
    B = 2 if DL % 256 == 0 and NV % 4 == 0 else 1
    A = NV // B
    H = DL // B
    W = min(H, 256)
    NH = H // W
    F = 2
    C = NH * B * F
    Q = R // F
    pred_scale = float(np.float32(1.0) / np.sqrt(np.float32(X * NV)))
    grad_scale = float(np.sqrt(np.float32(X * NV)) / np.float32(R * NV * DL * NO))
    bf, f32 = jnp.bfloat16, jnp.float32
    dma = pltpu.SemaphoreType.DMA
    vmem = pl.BlockSpec(memory_space=pltpu.VMEM)
    mu, weighted = pl.pallas_call(
        functools.partial(kernel, A, B, NO, W, pred_scale, grad_scale),
        out_shape=(
            jax.ShapeDtypeStruct((1, X), f32),
            jax.ShapeDtypeStruct((R, DL), f32),
        ),
        in_specs=[pl.BlockSpec(memory_space=pl.ANY)] * 5 + [vmem],
        out_specs=(vmem, vmem),
        scratch_shapes=[
            pltpu.VMEM((A * B, R, B * X), bf),
            pltpu.VMEM((H, B * X), bf),
            pltpu.VMEM((B, R, H), f32),
            pltpu.VMEM((R, DL), jnp.int32),
            pltpu.VMEM((R, DL), jnp.int32),
            pltpu.VMEM((R, DL), bf),
            pltpu.VMEM((B, R, H), bf),
            pltpu.VMEM((1, B * X), f32),
            pltpu.VMEM((W, B * X), bf),
            pltpu.VMEM((C, A, Q, W), f32),
            pltpu.VMEM((C, A, Q, W), bf),
            pltpu.VMEM((ITERS, C, A, Q, W), bf),
            pltpu.VMEM((ITERS, C, 2, Q, W), bf),
            pltpu.VMEM((ITERS, C, A, Q, W), bf),
            pltpu.VMEM((NH, B, R, W), f32),
            pltpu.VMEM((NH, B, R, W), f32),
            pltpu.VMEM((ITERS, B * NO, 1, B * X), f32),
            dma((B,)), dma((B,)),
            dma((NO // 2, B)), dma((NO // 2, B)),
            dma((NO // 2, B)), dma((NO // 2, B)),
            dma((NH, B)), dma((NH, B)),
            dma((3, B)), dma((3, B)),
            dma((NH, B)), dma((NH, B)),
            dma((C, A)), dma((ITERS, C, A)), dma((C,)), dma((ITERS, C)), dma((C, A)),
            dma((C, A)), dma((ITERS, C, A)),
            dma((B * NO,)), dma((ITERS, B * NO)),
            dma((4 + NH,)),
        ],
        compiler_params=pltpu.CompilerParams(
            collective_id=0, has_side_effects=True, vmem_limit_bytes=63 * 1024 * 1024
        ),
    )(
        source_fields.reshape(q, R, X), detector_fields, measured, valid_pair, weight_class,
        absorption.reshape(1, X),
    )
    return mu.reshape(X), weighted


def solution(mesh):
    placed = (
        P("opt", "vox"),
        P("opt", "vox"),
        P("vox", "opt"),
        P("vox", "opt"),
        P("vox", "opt"),
        P("vox"),
    )
    return jax.shard_map(
        local, mesh=mesh, in_specs=placed, out_specs=(P("vox"), P("vox", "opt")), check_vma=False
    )
```

```python
import functools

import jax
import jax.numpy as jnp
import numpy as np
from jax import lax
from jax.experimental import pallas as pl
from jax.experimental.pallas import tpu as pltpu
from jax.sharding import PartitionSpec as P

ITERS = 2
MESH = pl.DeviceIdType.MESH


def kernel(
    A, B, NO, W, pred_scale, grad_scale,
    s_in, d_in, meas_in, valid_in, class_in, mu_in,
    mu_out, res_ref,
    s_full, d_full, meas_ref, valid_ref, class_ref, codes, code_ref, mu_ref, scaled,
    own, zsend, zrecv, zrel, wfull, rsend, rrecv, gbuf,
    sy_send, sy_recv, sx_send, sx_recv, sm_send, sm_recv, d_send, d_recv,
    p_send, p_recv, r_send, r_recv, z_send, z_recv, rel_send, rel_recv, h_send, w_send, w_recv, g_send, g_recv, in_sem,
):
    q, R, X = s_in.shape
    H = d_in.shape[0] // B
    NH = H // W
    F = 2
    C = NH * B * F
    Q = R // F
    vox = lax.axis_index("vox")
    opt = lax.axis_index("opt")
    z, y = vox // B, lax.rem(vox, B)
    chip, core = opt // 2, lax.rem(opt, 2)
    NC = NO // 2
    mate = chip * 2 + 1 - core
    rows_y = [lax.rem(y + k, B) for k in range(B)]
    y_peers = rows_y[1:]
    z_peers = [lax.rem(z + k, A) for k in range(1, A)]
    line = A == 4
    inner = lax.rem((z + 1) // 2, 2)
    near = inner * 3 * (z - 1) + (1 - inner) * (1 + z // 3)
    across = 2 - z // 2
    base = 2 * (1 - z // 2)
    z_direct = [near] if line else z_peers
    z_adds = [near, across] if line else z_peers
    c_peers = [lax.rem(chip + k, NC) for k in range(1, NC)]
    group = [
        (lax.rem(y + k, B), lax.rem(opt + j, NO)) for k in range(B) for j in range(NO) if k + j > 0
    ]

    def remote(src, dst, send, recv, where):
        return pltpu.make_async_remote_copy(
            src_ref=src, dst_ref=dst, send_sem=send, recv_sem=recv,
            device_id=where, device_id_type=MESH,
        )

    def half(yy):
        return pl.ds(pl.multiple_of(yy * X, X), X)

    def cols(yy):
        return pl.ds(pl.multiple_of(yy * H, H), H)

    def at_y(p):
        return {"vox": z * B + p}

    def at_z(t):
        return {"vox": t * B + y}

    def block(j, yy):
        return s_full.at[pl.ds(j * q, q), :, half(yy)]

    def d_block(h, yy):
        return d_full.at[pl.ds(h * W, W), half(yy)]

    def d_rows(h, yy):
        return d_in.at[pl.ds(pl.multiple_of(yy * H + h * W, W), W)]

    loads = [
        pltpu.make_async_copy(valid_in, valid_ref, in_sem.at[0]),
        pltpu.make_async_copy(class_in, class_ref, in_sem.at[1]),
        pltpu.make_async_copy(s_in, block(opt, y), in_sem.at[2]),
        pltpu.make_async_copy(meas_in.at[:, cols(y)], meas_ref.at[y], in_sem.at[3]),
    ] + [
        pltpu.make_async_copy(d_rows(h, y), d_block(h, y), in_sem.at[4 + h]) for h in range(NH)
    ]
    for load in loads:
        load.start()

    barrier = pltpu.get_barrier_semaphore()
    for t in z_peers:
        pl.semaphore_signal(barrier, inc=1, device_id=at_z(t), device_id_type=MESH)
    for p, j in group:
        pl.semaphore_signal(
            barrier, inc=1, device_id={"vox": z * B + p, "opt": j}, device_id_type=MESH
        )
    pl.semaphore_wait(barrier, A - 1 + B * NO - 1)

    def s_y(p, yy):
        return remote(s_in, block(opt, yy), sy_send.at[p], sy_recv.at[yy], at_y(p))

    def s_x(p, j, yy):
        return remote(
            block(j, yy), block(j, yy), sx_send.at[p, yy], sx_recv.at[j // 2, yy],
            {"opt": p * 2 + core},
        )

    def s_x_own(p):
        return remote(
            s_in, block(opt, y), sx_send.at[p, y], sx_recv.at[chip, y], {"opt": p * 2 + core}
        )

    def s_m(p, cc, yy):
        mine = block(p * 2 + cc, yy)
        return remote(mine, mine, sm_send.at[p, yy], sm_recv.at[p, yy], {"opt": mate})

    def s_m_own():
        return remote(s_in, block(opt, y), sm_send.at[chip, y], sm_recv.at[chip, y], {"opt": mate})

    def d_y(h, p, yy):
        return remote(d_rows(h, p), d_block(h, yy), d_send.at[h, p], d_recv.at[h, yy], at_y(p))

    def pairs(p, yy):
        return [
            remote(mu_in, mu_ref.at[:, half(yy)], p_send.at[0, p], p_recv.at[0, yy], at_y(p)),
            remote(
                meas_in.at[:, cols(p)], meas_ref.at[yy], p_send.at[1, p], p_recv.at[1, yy], at_y(p)
            ),
            remote(
                codes.at[:, cols(p)], code_ref.at[yy], p_send.at[2, p], p_recv.at[2, yy], at_y(p)
            ),
        ]

    for p in y_peers:
        s_y(p, y).start()
    for p in c_peers:
        s_x_own(p).start()
    s_m_own().start()
    for p in y_peers:
        pairs(p, y)[0].start()
    for load in loads:
        load.wait()
    mu_ref[:, half(y)] = mu_in[...]
    codes[...] = (valid_ref[...] * (1 + class_ref[...])).astype(jnp.float32).astype(jnp.bfloat16)
    code_ref[y] = codes[:, cols(y)]
    for p in y_peers:
        s_y(p, p).wait_recv()
        d_y(0, p, y).start()
        for pp in c_peers:
            s_x(pp, opt, p).start()
        s_m(chip, core, p).start()
    for yy in rows_y:
        for p in c_peers:
            s_x(p, p * 2 + core, yy).wait_recv()
            s_m(p, core, yy).start()
    for p in y_peers:
        for copy in pairs(p, y)[1:]:
            copy.start()
        for h in range(1, NH):
            d_y(h, p, y).start()
    for yy in rows_y:
        for p in range(NC):
            s_m(p, 1 - core, yy).wait_recv()
    for p in y_peers:
        pairs(p, p)[0].wait_recv()
        s_y(p, y).wait_send()
    for p in c_peers:
        s_x_own(p).wait_send()
        for yy in y_peers:
            s_x(p, opt, yy).wait_send()
    for p in range(NC):
        for yy in rows_y:
            s_m(p, core, yy).wait_send()

    def back(h, p, yy):
        return remote(
            rsend.at[h, p], rrecv.at[h, yy], r_send.at[h, p], r_recv.at[h, yy], at_y(p)
        )

    def step(it, carry):
        def z_copy(c, t, src):
            return remote(
                zsend.at[c, t], zrecv.at[it, c, src], z_send.at[c, t], z_recv.at[it, c, src], at_z(t)
            )

        def rel_copy(c):
            return remote(
                zsend.at[c, pl.ds(base, 2)], zrel.at[it, c], rel_send.at[c], rel_recv.at[it, c],
                at_z(near),
            )

        def hand_on(c, src):
            mine = wfull.at[it, c, src]
            return remote(mine, mine, h_send.at[c, src], w_recv.at[it, c, src], at_z(near))

        def w_copy(c, t, src):
            mine = wfull.at[it, c, src]
            return remote(mine, mine, w_send.at[c, t], w_recv.at[it, c, src], at_z(t))

        def rows_of(c):
            r, f = rows_y[c // F % B], c % F
            return jnp.concatenate(
                [s_full[a * B + r, pl.ds(f * Q, Q)] for a in range(A)], axis=0
            )

        def predict(c):
            h, r = c // (B * F), rows_y[c // F % B]
            if c % (B * F) == 0:
                @pl.when(it == 0)
                def _():
                    for p in y_peers:
                        d_y(h, p, p).wait_recv()

                scaled[...] = (
                    d_full[pl.ds(h * W, W)].astype(jnp.float32) * mu_ref[...]
                ).astype(jnp.bfloat16).T
            rows = rows_of(c)
            part = jnp.dot(rows, scaled[...], preferred_element_type=jnp.float32).reshape(A, Q, W)
            zsend[c] = part.astype(jnp.bfloat16)
            for t in z_direct:
                z_copy(c, t, z).start()
            if line:
                @pl.when(inner == 0)
                def _():
                    rel_copy(c).start()
            own[c] = part

        def relay(c):
            if line:
                @pl.when(inner == 1)
                def _():
                    rel_copy(c).wait_recv()
                    both = pl.ds(base, 2)
                    total = own[c, both] + zrel[it, c].astype(jnp.float32)
                    zsend[c, both] = total.astype(jnp.bfloat16)
                    for k in range(2):
                        z_copy(c, base + k, z).start()

        def forward(c):
            if line:
                @pl.when(inner == 1)
                def _():
                    for k in range(2):
                        w_copy(c, base + k, base + k).wait_recv()
                        hand_on(c, base + k).start()

        def over_z(c):
            h, k, f = c // (B * F), c // F % B, c % F
            r = rows_y[k]
            if h == 0 and k > 0 and f == 0:
                @pl.when(it == 0)
                def _():
                    for copy in pairs(r, r)[1:]:
                        copy.wait_recv()

            total = own[c, z]
            for t in z_adds:
                z_copy(c, t, t).wait_recv()
                total = total + zrecv[it, c, t].astype(jnp.float32)
            here, part = pl.ds(h * W, W), pl.ds(f * Q, Q)
            code = code_ref[r, part, here].astype(jnp.float32)
            weight = jnp.where(code > 0.0, 1.0 / jnp.maximum(code, 1.0), 0.0)
            weighted = weight * (total * pred_scale - meas_ref[r, part, here])
            wfull[it, c, z] = weighted.astype(jnp.bfloat16)
            for t in z_adds:
                w_copy(c, t, z).start()
            rsend[h, r, part] = weighted
            if k > 0 and f == F - 1:
                @pl.when(it == ITERS - 1)
                def _():
                    back(h, r, y).start()

        def gradient(c, total):
            h = c // (B * F)
            for t in z_direct:
                w_copy(c, t, t).wait_recv()
            if line:
                @pl.when(inner == 0)
                def _():
                    for k in range(2):
                        w_copy(c, base + k, base + k).wait_recv()
            w = wfull[it, c].reshape(A * Q, W)
            summed = jnp.dot(w, d_full[pl.ds(h * W, W)], preferred_element_type=jnp.float32)
            summed = summed * rows_of(c).astype(jnp.float32)
            return total + jnp.sum(summed.reshape(A * Q // 8, 8, B * X), axis=0)

        total = jnp.zeros((8, B * X), jnp.float32)
        for c in range(min(2, C)):
            predict(c)
        relay(0)
        for slot in range(C + 3):
            if slot + 2 < C:
                predict(slot + 2)
            if slot + 1 < C:
                relay(slot + 1)
            if slot < C:
                over_z(slot)
            if 0 < slot <= C:
                forward(slot - 1)
            if slot > 2:
                total = gradient(slot - 3, total)

        def g_copy(p, j, sp, sj):
            mine = gbuf.at[it, sp * NO + sj]
            return remote(
                mine, mine, g_send.at[p * NO + j], g_recv.at[it, sp * NO + sj],
                {"vox": z * B + p, "opt": j},
            )

        gbuf[it, y * NO + opt] = jnp.sum(total, axis=0, keepdims=True)
        for p, j in group:
            g_copy(p, j, y, opt).start()
        for c in range(C):
            for t in z_direct:
                z_copy(c, t, z).wait_send()
            for t in z_adds:
                w_copy(c, t, z).wait_send()
            if line:
                @pl.when(inner == 1)
                def _():
                    for k in range(2):
                        z_copy(c, base + k, z).wait_send()
                        hand_on(c, base + k).wait_send()

                @pl.when(inner == 0)
                def _():
                    rel_copy(c).wait_send()
        for p, j in group:
            g_copy(p, j, p, j).wait_recv()
        grad = gbuf[it, 0]
        for j in range(1, B * NO):
            grad = grad + gbuf[it, j]
        mu_ref[...] = jnp.maximum(mu_ref[...] - 2.0 * (grad * grad_scale), 0.0)
        for p, j in group:
            g_copy(p, j, y, opt).wait_send()
        return carry

    lax.fori_loop(0, ITERS, step, 0)
    mu_out[...] = mu_ref[:, half(y)]
    for h in range(NH):
        res_ref[:, pl.ds(pl.multiple_of(y * H + h * W, W), W)] = rsend[h, y]
        for p in y_peers:
            back(h, p, p).wait_recv()
            res_ref[:, pl.ds(pl.multiple_of(p * H + h * W, W), W)] = rrecv[h, p]
            back(h, p, y).wait_send()
            d_y(h, p, y).wait_send()
    for p in y_peers:
        for copy in pairs(p, y):
            copy.wait_send()


def local(source_fields, detector_fields, measured, valid_pair, weight_class, absorption):
    NV, NO = lax.axis_size("vox"), lax.axis_size("opt")
    R, DL = measured.shape
    X = absorption.shape[0]
    q = source_fields.shape[0] // R
    B = 2 if DL % 256 == 0 and NV % 4 == 0 else 1
    A = NV // B
    H = DL // B
    W = min(H, 256)
    NH = H // W
    F = 2
    C = NH * B * F
    Q = R // F
    pred_scale = float(np.float32(1.0) / np.sqrt(np.float32(X * NV)))
    grad_scale = float(np.sqrt(np.float32(X * NV)) / np.float32(R * NV * DL * NO))
    bf, f32 = jnp.bfloat16, jnp.float32
    dma = pltpu.SemaphoreType.DMA
    vmem = pl.BlockSpec(memory_space=pltpu.VMEM)
    mu, weighted = pl.pallas_call(
        functools.partial(kernel, A, B, NO, W, pred_scale, grad_scale),
        out_shape=(
            jax.ShapeDtypeStruct((1, X), f32),
            jax.ShapeDtypeStruct((R, DL), f32),
        ),
        in_specs=[pl.BlockSpec(memory_space=pl.ANY)] * 5 + [vmem],
        out_specs=(vmem, vmem),
        scratch_shapes=[
            pltpu.VMEM((A * B, R, B * X), bf),
            pltpu.VMEM((H, B * X), bf),
            pltpu.VMEM((B, R, H), f32),
            pltpu.VMEM((R, DL), jnp.int32),
            pltpu.VMEM((R, DL), jnp.int32),
            pltpu.VMEM((R, DL), bf),
            pltpu.VMEM((B, R, H), bf),
            pltpu.VMEM((1, B * X), f32),
            pltpu.VMEM((B * X, W), bf),
            pltpu.VMEM((C, A, Q, W), f32),
            pltpu.VMEM((C, A, Q, W), bf),
            pltpu.VMEM((ITERS, C, A, Q, W), bf),
            pltpu.VMEM((ITERS, C, 2, Q, W), bf),
            pltpu.VMEM((ITERS, C, A, Q, W), bf),
            pltpu.VMEM((NH, B, R, W), f32),
            pltpu.VMEM((NH, B, R, W), f32),
            pltpu.VMEM((ITERS, B * NO, 1, B * X), f32),
            dma((B,)), dma((B,)),
            dma((NO // 2, B)), dma((NO // 2, B)),
            dma((NO // 2, B)), dma((NO // 2, B)),
            dma((NH, B)), dma((NH, B)),
            dma((3, B)), dma((3, B)),
            dma((NH, B)), dma((NH, B)),
            dma((C, A)), dma((ITERS, C, A)), dma((C,)), dma((ITERS, C)), dma((C, A)),
            dma((C, A)), dma((ITERS, C, A)),
            dma((B * NO,)), dma((ITERS, B * NO)),
            dma((4 + NH,)),
        ],
        compiler_params=pltpu.CompilerParams(
            collective_id=0, has_side_effects=True, vmem_limit_bytes=63 * 1024 * 1024
        ),
    )(
        source_fields.reshape(q, R, X), detector_fields, measured, valid_pair, weight_class,
        absorption.reshape(1, X),
    )
    return mu.reshape(X), weighted


def solution(mesh):
    placed = (
        P("opt", "vox"),
        P("opt", "vox"),
        P("vox", "opt"),
        P("vox", "opt"),
        P("vox", "opt"),
        P("vox"),
    )
    return jax.shard_map(
        local, mesh=mesh, in_specs=placed, out_specs=(P("vox"), P("vox", "opt")), check_vma=False
    )
```

```python
import functools

import jax
import jax.numpy as jnp
import numpy as np
from jax import lax
from jax.experimental import pallas as pl
from jax.experimental.pallas import tpu as pltpu
from jax.sharding import PartitionSpec as P

ITERS = 2
MESH = pl.DeviceIdType.MESH


def kernel(
    A, B, NO, W, pred_scale, grad_scale,
    s_in, d_in, meas_in, valid_in, class_in, mu_in,
    mu_out, res_ref,
    s_full, d_full, meas_ref, valid_ref, class_ref, codes, code_ref, mu_ref, scaled,
    own, zsend, zrecv, zrel, wfull, rsend, rrecv, gbuf,
    sy_send, sy_recv, sx_send, sx_recv, sm_send, sm_recv, d_send, d_recv,
    p_send, p_recv, r_send, r_recv, z_send, z_recv, rel_send, rel_recv, h_send, w_send, w_recv, g_send, g_recv, in_sem,
):
    q, R, X = s_in.shape
    H = d_in.shape[0] // B
    NH = H // W
    F = 1
    C = NH * B * F
    Q = R // F
    vox = lax.axis_index("vox")
    opt = lax.axis_index("opt")
    z, y = vox // B, lax.rem(vox, B)
    chip, core = opt // 2, lax.rem(opt, 2)
    NC = NO // 2
    mate = chip * 2 + 1 - core
    rows_y = [lax.rem(y + k, B) for k in range(B)]
    y_peers = rows_y[1:]
    z_peers = [lax.rem(z + k, A) for k in range(1, A)]
    line = A == 4
    inner = lax.rem((z + 1) // 2, 2)
    near = inner * 3 * (z - 1) + (1 - inner) * (1 + z // 3)
    across = 2 - z // 2
    base = 2 * (1 - z // 2)
    z_direct = [near] if line else z_peers
    z_adds = [near, across] if line else z_peers
    c_peers = [lax.rem(chip + k, NC) for k in range(1, NC)]
    group = [
        (lax.rem(y + k, B), lax.rem(opt + j, NO)) for k in range(B) for j in range(NO) if k + j > 0
    ]

    def remote(src, dst, send, recv, where):
        return pltpu.make_async_remote_copy(
            src_ref=src, dst_ref=dst, send_sem=send, recv_sem=recv,
            device_id=where, device_id_type=MESH,
        )

    def half(yy):
        return pl.ds(pl.multiple_of(yy * X, X), X)

    def cols(yy):
        return pl.ds(pl.multiple_of(yy * H, H), H)

    def at_y(p):
        return {"vox": z * B + p}

    def at_z(t):
        return {"vox": t * B + y}

    def block(j, yy):
        return s_full.at[pl.ds(j * q, q), :, half(yy)]

    def d_block(h, yy):
        return d_full.at[pl.ds(h * W, W), half(yy)]

    def d_rows(h, yy):
        return d_in.at[pl.ds(pl.multiple_of(yy * H + h * W, W), W)]

    loads = [
        pltpu.make_async_copy(valid_in, valid_ref, in_sem.at[0]),
        pltpu.make_async_copy(class_in, class_ref, in_sem.at[1]),
        pltpu.make_async_copy(s_in, block(opt, y), in_sem.at[2]),
        pltpu.make_async_copy(meas_in.at[:, cols(y)], meas_ref.at[y], in_sem.at[3]),
    ] + [
        pltpu.make_async_copy(d_rows(h, y), d_block(h, y), in_sem.at[4 + h]) for h in range(NH)
    ]
    for load in loads:
        load.start()

    barrier = pltpu.get_barrier_semaphore()
    for t in z_peers:
        pl.semaphore_signal(barrier, inc=1, device_id=at_z(t), device_id_type=MESH)
    for p, j in group:
        pl.semaphore_signal(
            barrier, inc=1, device_id={"vox": z * B + p, "opt": j}, device_id_type=MESH
        )
    pl.semaphore_wait(barrier, A - 1 + B * NO - 1)

    def s_y(p, yy):
        return remote(s_in, block(opt, yy), sy_send.at[p], sy_recv.at[yy], at_y(p))

    def s_x(p, j, yy):
        return remote(
            block(j, yy), block(j, yy), sx_send.at[p, yy], sx_recv.at[j // 2, yy],
            {"opt": p * 2 + core},
        )

    def s_x_own(p):
        return remote(
            s_in, block(opt, y), sx_send.at[p, y], sx_recv.at[chip, y], {"opt": p * 2 + core}
        )

    def s_m(p, cc, yy):
        mine = block(p * 2 + cc, yy)
        return remote(mine, mine, sm_send.at[p, yy], sm_recv.at[p, yy], {"opt": mate})

    def s_m_own():
        return remote(s_in, block(opt, y), sm_send.at[chip, y], sm_recv.at[chip, y], {"opt": mate})

    def d_y(h, p, yy):
        return remote(d_rows(h, p), d_block(h, yy), d_send.at[h, p], d_recv.at[h, yy], at_y(p))

    def pairs(p, yy):
        return [
            remote(mu_in, mu_ref.at[:, half(yy)], p_send.at[0, p], p_recv.at[0, yy], at_y(p)),
            remote(
                meas_in.at[:, cols(p)], meas_ref.at[yy], p_send.at[1, p], p_recv.at[1, yy], at_y(p)
            ),
            remote(
                codes.at[:, cols(p)], code_ref.at[yy], p_send.at[2, p], p_recv.at[2, yy], at_y(p)
            ),
        ]

    for p in y_peers:
        s_y(p, y).start()
    for p in c_peers:
        s_x_own(p).start()
    s_m_own().start()
    for p in y_peers:
        pairs(p, y)[0].start()
    for load in loads:
        load.wait()
    mu_ref[:, half(y)] = mu_in[...]
    codes[...] = (valid_ref[...] * (1 + class_ref[...])).astype(jnp.float32).astype(jnp.bfloat16)
    code_ref[y] = codes[:, cols(y)]
    for p in y_peers:
        s_y(p, p).wait_recv()
        d_y(0, p, y).start()
        for pp in c_peers:
            s_x(pp, opt, p).start()
        s_m(chip, core, p).start()
    for yy in rows_y:
        for p in c_peers:
            s_x(p, p * 2 + core, yy).wait_recv()
            s_m(p, core, yy).start()
    for p in y_peers:
        for copy in pairs(p, y)[1:]:
            copy.start()
        for h in range(1, NH):
            d_y(h, p, y).start()
    for yy in rows_y:
        for p in range(NC):
            s_m(p, 1 - core, yy).wait_recv()
    for p in y_peers:
        pairs(p, p)[0].wait_recv()
        s_y(p, y).wait_send()
    for p in c_peers:
        s_x_own(p).wait_send()
        for yy in y_peers:
            s_x(p, opt, yy).wait_send()
    for p in range(NC):
        for yy in rows_y:
            s_m(p, core, yy).wait_send()

    def back(h, p, yy):
        return remote(
            rsend.at[h, p], rrecv.at[h, yy], r_send.at[h, p], r_recv.at[h, yy], at_y(p)
        )

    def step(it, carry):
        def z_copy(c, t, src):
            return remote(
                zsend.at[c, t], zrecv.at[it, c, src], z_send.at[c, t], z_recv.at[it, c, src], at_z(t)
            )

        def rel_copy(c):
            return remote(
                zsend.at[c, pl.ds(base, 2)], zrel.at[it, c], rel_send.at[c], rel_recv.at[it, c],
                at_z(near),
            )

        def hand_on(c, src):
            mine = wfull.at[it, c, src]
            return remote(mine, mine, h_send.at[c, src], w_recv.at[it, c, src], at_z(near))

        def w_copy(c, t, src):
            mine = wfull.at[it, c, src]
            return remote(mine, mine, w_send.at[c, t], w_recv.at[it, c, src], at_z(t))

        def rows_of(c):
            r, f = rows_y[c // F % B], c % F
            return jnp.concatenate(
                [s_full[a * B + r, pl.ds(f * Q, Q)] for a in range(A)], axis=0
            )

        def predict(c):
            h, r = c // (B * F), rows_y[c // F % B]
            if c % (B * F) == 0:
                @pl.when(it == 0)
                def _():
                    for p in y_peers:
                        d_y(h, p, p).wait_recv()

                scaled[...] = (
                    d_full[pl.ds(h * W, W)].astype(jnp.float32) * mu_ref[...]
                ).astype(jnp.bfloat16).T
            rows = rows_of(c)
            part = jnp.dot(rows, scaled[...], preferred_element_type=jnp.float32).reshape(A, Q, W)
            zsend[c] = part.astype(jnp.bfloat16)
            for t in z_direct:
                z_copy(c, t, z).start()
            if line:
                @pl.when(inner == 0)
                def _():
                    rel_copy(c).start()
            own[c] = part

        def relay(c):
            if line:
                @pl.when(inner == 1)
                def _():
                    rel_copy(c).wait_recv()
                    both = pl.ds(base, 2)
                    total = own[c, both] + zrel[it, c].astype(jnp.float32)
                    zsend[c, both] = total.astype(jnp.bfloat16)
                    for k in range(2):
                        z_copy(c, base + k, z).start()

        def forward(c):
            if line:
                @pl.when(inner == 1)
                def _():
                    for k in range(2):
                        w_copy(c, base + k, base + k).wait_recv()
                        hand_on(c, base + k).start()

        def over_z(c):
            h, k, f = c // (B * F), c // F % B, c % F
            r = rows_y[k]
            if h == 0 and k > 0 and f == 0:
                @pl.when(it == 0)
                def _():
                    for copy in pairs(r, r)[1:]:
                        copy.wait_recv()

            total = own[c, z]
            for t in z_adds:
                z_copy(c, t, t).wait_recv()
                total = total + zrecv[it, c, t].astype(jnp.float32)
            here, part = pl.ds(h * W, W), pl.ds(f * Q, Q)
            code = code_ref[r, part, here].astype(jnp.float32)
            weight = jnp.where(code > 0.0, 1.0 / jnp.maximum(code, 1.0), 0.0)
            weighted = weight * (total * pred_scale - meas_ref[r, part, here])
            wfull[it, c, z] = weighted.astype(jnp.bfloat16)
            for t in z_adds:
                w_copy(c, t, z).start()
            rsend[h, r, part] = weighted
            if k > 0 and f == F - 1:
                @pl.when(it == ITERS - 1)
                def _():
                    back(h, r, y).start()

        def gradient(c, total):
            h = c // (B * F)
            for t in z_direct:
                w_copy(c, t, t).wait_recv()
            if line:
                @pl.when(inner == 0)
                def _():
                    for k in range(2):
                        w_copy(c, base + k, base + k).wait_recv()
            w = wfull[it, c].reshape(A * Q, W)
            summed = jnp.dot(w, d_full[pl.ds(h * W, W)], preferred_element_type=jnp.float32)
            summed = summed * rows_of(c).astype(jnp.float32)
            return total + jnp.sum(summed.reshape(A * Q // 8, 8, B * X), axis=0)

        total = jnp.zeros((8, B * X), jnp.float32)
        for c in range(min(2, C)):
            predict(c)
        relay(0)
        for slot in range(C + 3):
            if slot + 2 < C:
                predict(slot + 2)
            if slot + 1 < C:
                relay(slot + 1)
            if slot < C:
                over_z(slot)
            if 0 < slot <= C:
                forward(slot - 1)
            if slot > 2:
                total = gradient(slot - 3, total)

        def g_copy(p, j, sp, sj):
            mine = gbuf.at[it, sp * NO + sj]
            return remote(
                mine, mine, g_send.at[p * NO + j], g_recv.at[it, sp * NO + sj],
                {"vox": z * B + p, "opt": j},
            )

        gbuf[it, y * NO + opt] = jnp.sum(total, axis=0, keepdims=True)
        for p, j in group:
            g_copy(p, j, y, opt).start()
        for c in range(C):
            for t in z_direct:
                z_copy(c, t, z).wait_send()
            for t in z_adds:
                w_copy(c, t, z).wait_send()
            if line:
                @pl.when(inner == 1)
                def _():
                    for k in range(2):
                        z_copy(c, base + k, z).wait_send()
                        hand_on(c, base + k).wait_send()

                @pl.when(inner == 0)
                def _():
                    rel_copy(c).wait_send()
        for p, j in group:
            g_copy(p, j, p, j).wait_recv()
        grad = gbuf[it, 0]
        for j in range(1, B * NO):
            grad = grad + gbuf[it, j]
        mu_ref[...] = jnp.maximum(mu_ref[...] - 2.0 * (grad * grad_scale), 0.0)
        for p, j in group:
            g_copy(p, j, y, opt).wait_send()
        return carry

    lax.fori_loop(0, ITERS, step, 0)
    mu_out[...] = mu_ref[:, half(y)]
    for h in range(NH):
        res_ref[:, pl.ds(pl.multiple_of(y * H + h * W, W), W)] = rsend[h, y]
        for p in y_peers:
            back(h, p, p).wait_recv()
            res_ref[:, pl.ds(pl.multiple_of(p * H + h * W, W), W)] = rrecv[h, p]
            back(h, p, y).wait_send()
            d_y(h, p, y).wait_send()
    for p in y_peers:
        for copy in pairs(p, y):
            copy.wait_send()


def local(source_fields, detector_fields, measured, valid_pair, weight_class, absorption):
    NV, NO = lax.axis_size("vox"), lax.axis_size("opt")
    R, DL = measured.shape
    X = absorption.shape[0]
    q = source_fields.shape[0] // R
    B = 2 if DL % 256 == 0 and NV % 4 == 0 else 1
    A = NV // B
    H = DL // B
    W = min(H, 256)
    NH = H // W
    F = 1
    C = NH * B * F
    Q = R // F
    pred_scale = float(np.float32(1.0) / np.sqrt(np.float32(X * NV)))
    grad_scale = float(np.sqrt(np.float32(X * NV)) / np.float32(R * NV * DL * NO))
    bf, f32 = jnp.bfloat16, jnp.float32
    dma = pltpu.SemaphoreType.DMA
    vmem = pl.BlockSpec(memory_space=pltpu.VMEM)
    mu, weighted = pl.pallas_call(
        functools.partial(kernel, A, B, NO, W, pred_scale, grad_scale),
        out_shape=(
            jax.ShapeDtypeStruct((1, X), f32),
            jax.ShapeDtypeStruct((R, DL), f32),
        ),
        in_specs=[pl.BlockSpec(memory_space=pl.ANY)] * 5 + [vmem],
        out_specs=(vmem, vmem),
        scratch_shapes=[
            pltpu.VMEM((A * B, R, B * X), bf),
            pltpu.VMEM((H, B * X), bf),
            pltpu.VMEM((B, R, H), f32),
            pltpu.VMEM((R, DL), jnp.int32),
            pltpu.VMEM((R, DL), jnp.int32),
            pltpu.VMEM((R, DL), bf),
            pltpu.VMEM((B, R, H), bf),
            pltpu.VMEM((1, B * X), f32),
            pltpu.VMEM((B * X, W), bf),
            pltpu.VMEM((C, A, Q, W), f32),
            pltpu.VMEM((C, A, Q, W), bf),
            pltpu.VMEM((ITERS, C, A, Q, W), bf),
            pltpu.VMEM((ITERS, C, 2, Q, W), bf),
            pltpu.VMEM((ITERS, C, A, Q, W), bf),
            pltpu.VMEM((NH, B, R, W), f32),
            pltpu.VMEM((NH, B, R, W), f32),
            pltpu.VMEM((ITERS, B * NO, 1, B * X), f32),
            dma((B,)), dma((B,)),
            dma((NO // 2, B)), dma((NO // 2, B)),
            dma((NO // 2, B)), dma((NO // 2, B)),
            dma((NH, B)), dma((NH, B)),
            dma((3, B)), dma((3, B)),
            dma((NH, B)), dma((NH, B)),
            dma((C, A)), dma((ITERS, C, A)), dma((C,)), dma((ITERS, C)), dma((C, A)),
            dma((C, A)), dma((ITERS, C, A)),
            dma((B * NO,)), dma((ITERS, B * NO)),
            dma((4 + NH,)),
        ],
        compiler_params=pltpu.CompilerParams(
            collective_id=0, has_side_effects=True, vmem_limit_bytes=63 * 1024 * 1024
        ),
    )(
        source_fields.reshape(q, R, X), detector_fields, measured, valid_pair, weight_class,
        absorption.reshape(1, X),
    )
    return mu.reshape(X), weighted


def solution(mesh):
    placed = (
        P("opt", "vox"),
        P("opt", "vox"),
        P("vox", "opt"),
        P("vox", "opt"),
        P("vox", "opt"),
        P("vox"),
    )
    return jax.shard_map(
        local, mesh=mesh, in_specs=placed, out_specs=(P("vox"), P("vox", "opt")), check_vma=False
    )
```

```python
import functools

import jax
import jax.numpy as jnp
import numpy as np
from jax import lax
from jax.experimental import pallas as pl
from jax.experimental.pallas import tpu as pltpu
from jax.sharding import PartitionSpec as P

ITERS = 2
MESH = pl.DeviceIdType.MESH


def kernel(
    A, B, NO, W, pred_scale, grad_scale,
    s_in, d_in, meas_in, valid_in, class_in, mu_in,
    mu_out, res_ref,
    s_full, d_full, meas_ref, valid_ref, class_ref, codes, code_ref, mu_ref, scaled,
    own, zsend, zrecv, zrel, wfull, rsend, rrecv, gbuf,
    sy_send, sy_recv, sx_send, sx_recv, sm_send, sm_recv, d_send, d_recv,
    p_send, p_recv, r_send, r_recv, z_send, z_recv, rel_send, rel_recv, h_send, w_send, w_recv, g_send, g_recv, in_sem,
):
    q, R, X = s_in.shape
    H = d_in.shape[0] // B
    NH = H // W
    F = 2
    C = NH * B * F
    Q = R // F
    vox = lax.axis_index("vox")
    opt = lax.axis_index("opt")
    z, y = vox // B, lax.rem(vox, B)
    chip, core = opt // 2, lax.rem(opt, 2)
    NC = NO // 2
    mate = chip * 2 + 1 - core
    rows_y = [lax.rem(y + k, B) for k in range(B)]
    y_peers = rows_y[1:]
    z_peers = [lax.rem(z + k, A) for k in range(1, A)]
    line = A == 4
    inner = lax.rem((z + 1) // 2, 2)
    near = inner * 3 * (z - 1) + (1 - inner) * (1 + z // 3)
    across = 2 - z // 2
    base = 2 * (1 - z // 2)
    z_direct = [near] if line else z_peers
    z_adds = [near, across] if line else z_peers
    c_peers = [lax.rem(chip + k, NC) for k in range(1, NC)]
    group = [
        (lax.rem(y + k, B), lax.rem(opt + j, NO)) for k in range(B) for j in range(NO) if k + j > 0
    ]

    def remote(src, dst, send, recv, where):
        return pltpu.make_async_remote_copy(
            src_ref=src, dst_ref=dst, send_sem=send, recv_sem=recv,
            device_id=where, device_id_type=MESH,
        )

    def half(yy):
        return pl.ds(pl.multiple_of(yy * X, X), X)

    def cols(yy):
        return pl.ds(pl.multiple_of(yy * H, H), H)

    def at_y(p):
        return {"vox": z * B + p}

    def at_z(t):
        return {"vox": t * B + y}

    def block(j, yy):
        return s_full.at[pl.ds(j * q, q), :, half(yy)]

    def d_block(h, yy):
        return d_full.at[pl.ds(h * W, W), half(yy)]

    def d_rows(h, yy):
        return d_in.at[pl.ds(pl.multiple_of(yy * H + h * W, W), W)]

    loads = [
        pltpu.make_async_copy(valid_in, valid_ref, in_sem.at[0]),
        pltpu.make_async_copy(class_in, class_ref, in_sem.at[1]),
        pltpu.make_async_copy(s_in, block(opt, y), in_sem.at[2]),
        pltpu.make_async_copy(meas_in.at[:, cols(y)], meas_ref.at[y], in_sem.at[3]),
    ] + [
        pltpu.make_async_copy(d_rows(h, y), d_block(h, y), in_sem.at[4 + h]) for h in range(NH)
    ]
    for load in loads:
        load.start()

    barrier = pltpu.get_barrier_semaphore()
    for t in z_peers:
        pl.semaphore_signal(barrier, inc=1, device_id=at_z(t), device_id_type=MESH)
    for p, j in group:
        pl.semaphore_signal(
            barrier, inc=1, device_id={"vox": z * B + p, "opt": j}, device_id_type=MESH
        )
    pl.semaphore_wait(barrier, A - 1 + B * NO - 1)

    def s_y(p, yy):
        return remote(s_in, block(opt, yy), sy_send.at[p], sy_recv.at[yy], at_y(p))

    def s_x(p, j, yy):
        return remote(
            block(j, yy), block(j, yy), sx_send.at[p, yy], sx_recv.at[j // 2, yy],
            {"opt": p * 2 + core},
        )

    def s_x_own(p):
        return remote(
            s_in, block(opt, y), sx_send.at[p, y], sx_recv.at[chip, y], {"opt": p * 2 + core}
        )

    def s_m(p, cc, yy):
        mine = block(p * 2 + cc, yy)
        return remote(mine, mine, sm_send.at[p, yy], sm_recv.at[p, yy], {"opt": mate})

    def s_m_own():
        return remote(s_in, block(opt, y), sm_send.at[chip, y], sm_recv.at[chip, y], {"opt": mate})

    def d_y(h, p, yy):
        return remote(d_rows(h, p), d_block(h, yy), d_send.at[h, p], d_recv.at[h, yy], at_y(p))

    def pairs(p, yy):
        return [
            remote(mu_in, mu_ref.at[:, half(yy)], p_send.at[0, p], p_recv.at[0, yy], at_y(p)),
            remote(
                meas_in.at[:, cols(p)], meas_ref.at[yy], p_send.at[1, p], p_recv.at[1, yy], at_y(p)
            ),
            remote(
                codes.at[:, cols(p)], code_ref.at[yy], p_send.at[2, p], p_recv.at[2, yy], at_y(p)
            ),
        ]

    for p in y_peers:
        s_y(p, y).start()
    for p in c_peers:
        s_x_own(p).start()
    s_m_own().start()
    for p in y_peers:
        pairs(p, y)[0].start()
    for load in loads:
        load.wait()
    mu_ref[:, half(y)] = mu_in[...]
    codes[...] = (valid_ref[...] * (1 + class_ref[...])).astype(jnp.float32).astype(jnp.bfloat16)
    code_ref[y] = codes[:, cols(y)]
    for p in y_peers:
        s_y(p, p).wait_recv()
        d_y(0, p, y).start()
        for pp in c_peers:
            s_x(pp, opt, p).start()
        s_m(chip, core, p).start()
    for yy in rows_y:
        for p in c_peers:
            s_x(p, p * 2 + core, yy).wait_recv()
            s_m(p, core, yy).start()
    for p in y_peers:
        for copy in pairs(p, y)[1:]:
            copy.start()
        for h in range(1, NH):
            d_y(h, p, y).start()
    for yy in rows_y:
        for p in range(NC):
            s_m(p, 1 - core, yy).wait_recv()
    for p in y_peers:
        pairs(p, p)[0].wait_recv()
        s_y(p, y).wait_send()
    for p in c_peers:
        s_x_own(p).wait_send()
        for yy in y_peers:
            s_x(p, opt, yy).wait_send()
    for p in range(NC):
        for yy in rows_y:
            s_m(p, core, yy).wait_send()

    def back(h, p, yy):
        return remote(
            rsend.at[h, p], rrecv.at[h, yy], r_send.at[h, p], r_recv.at[h, yy], at_y(p)
        )

    def step(it, carry):
        def z_copy(c, t, src):
            return remote(
                zsend.at[c, t], zrecv.at[it, c, src], z_send.at[c, t], z_recv.at[it, c, src], at_z(t)
            )

        def rel_copy(c):
            return remote(
                zsend.at[c, pl.ds(base, 2)], zrel.at[it, c], rel_send.at[c], rel_recv.at[it, c],
                at_z(near),
            )

        def hand_on(c, src):
            mine = wfull.at[it, c, src]
            return remote(mine, mine, h_send.at[c, src], w_recv.at[it, c, src], at_z(near))

        def w_copy(c, t, src):
            mine = wfull.at[it, c, src]
            return remote(mine, mine, w_send.at[c, t], w_recv.at[it, c, src], at_z(t))

        def rows_of(c):
            r, f = rows_y[c // F % B], c % F
            return jnp.concatenate(
                [s_full[a * B + r, pl.ds(f * Q, Q)] for a in range(A)], axis=0
            )

        def predict(c):
            h, r = c // (B * F), rows_y[c // F % B]
            if c % (B * F) == 0:
                @pl.when(it == 0)
                def _():
                    for p in y_peers:
                        d_y(h, p, p).wait_recv()

                scaled[...] = (
                    d_full[pl.ds(h * W, W)].astype(jnp.float32) * mu_ref[...]
                ).astype(jnp.bfloat16).T
            rows = rows_of(c)
            part = jnp.dot(rows, scaled[...], preferred_element_type=jnp.float32).reshape(A, Q, W)
            zsend[c] = part.astype(jnp.bfloat16)
            for t in z_direct:
                z_copy(c, t, z).start()
            if line:
                @pl.when(inner == 0)
                def _():
                    rel_copy(c).start()
            own[c] = part

        def relay(c):
            if line:
                @pl.when(inner == 1)
                def _():
                    rel_copy(c).wait_recv()
                    both = pl.ds(base, 2)
                    total = own[c, both] + zrel[it, c].astype(jnp.float32)
                    zsend[c, both] = total.astype(jnp.bfloat16)
                    for k in range(2):
                        z_copy(c, base + k, z).start()

        def forward(c):
            if line:
                @pl.when(inner == 1)
                def _():
                    for k in range(2):
                        w_copy(c, base + k, base + k).wait_recv()
                        hand_on(c, base + k).start()

        def over_z(c):
            h, k, f = c // (B * F), c // F % B, c % F
            r = rows_y[k]
            if h == 0 and k > 0 and f == 0:
                @pl.when(it == 0)
                def _():
                    for copy in pairs(r, r)[1:]:
                        copy.wait_recv()

            total = own[c, z]
            for t in z_adds:
                z_copy(c, t, t).wait_recv()
                total = total + zrecv[it, c, t].astype(jnp.float32)
            here, part = pl.ds(h * W, W), pl.ds(f * Q, Q)
            code = code_ref[r, part, here].astype(jnp.float32)
            weight = jnp.where(code > 0.0, 1.0 / jnp.maximum(code, 1.0), 0.0)
            weighted = weight * (total * pred_scale - meas_ref[r, part, here])
            wfull[it, c, z] = weighted.astype(jnp.bfloat16)
            for t in z_adds:
                w_copy(c, t, z).start()
            rsend[h, r, part] = weighted
            if k > 0 and f == F - 1:
                @pl.when(it == ITERS - 1)
                def _():
                    back(h, r, y).start()

        def gradient(c, total):
            h = c // (B * F)
            for t in z_direct:
                w_copy(c, t, t).wait_recv()
            if line:
                @pl.when(inner == 0)
                def _():
                    for k in range(2):
                        w_copy(c, base + k, base + k).wait_recv()
            w = wfull[it, c].reshape(A * Q, W)
            summed = jnp.dot(w, d_full[pl.ds(h * W, W)], preferred_element_type=jnp.float32)
            summed = summed * rows_of(c).astype(jnp.float32)
            return total + jnp.sum(summed.reshape(A * Q // 8, 8, B * X), axis=0)

        total = jnp.zeros((8, B * X), jnp.float32)
        for c in range(min(3, C)):
            predict(c)
        relay(0)
        for slot in range(C + 3):
            if slot + 1 < C:
                relay(slot + 1)
            if slot < C:
                over_z(slot)
            if 0 < slot <= C:
                forward(slot - 1)
            if slot + 3 < C:
                predict(slot + 3)
            if slot > 2:
                total = gradient(slot - 3, total)

        def g_copy(p, j, sp, sj):
            mine = gbuf.at[it, sp * NO + sj]
            return remote(
                mine, mine, g_send.at[p * NO + j], g_recv.at[it, sp * NO + sj],
                {"vox": z * B + p, "opt": j},
            )

        gbuf[it, y * NO + opt] = jnp.sum(total, axis=0, keepdims=True)
        for p, j in group:
            g_copy(p, j, y, opt).start()
        for c in range(C):
            for t in z_direct:
                z_copy(c, t, z).wait_send()
            for t in z_adds:
                w_copy(c, t, z).wait_send()
            if line:
                @pl.when(inner == 1)
                def _():
                    for k in range(2):
                        z_copy(c, base + k, z).wait_send()
                        hand_on(c, base + k).wait_send()

                @pl.when(inner == 0)
                def _():
                    rel_copy(c).wait_send()
        for p, j in group:
            g_copy(p, j, p, j).wait_recv()
        grad = gbuf[it, 0]
        for j in range(1, B * NO):
            grad = grad + gbuf[it, j]
        mu_ref[...] = jnp.maximum(mu_ref[...] - 2.0 * (grad * grad_scale), 0.0)
        for p, j in group:
            g_copy(p, j, y, opt).wait_send()
        return carry

    lax.fori_loop(0, ITERS, step, 0)
    mu_out[...] = mu_ref[:, half(y)]
    for h in range(NH):
        res_ref[:, pl.ds(pl.multiple_of(y * H + h * W, W), W)] = rsend[h, y]
        for p in y_peers:
            back(h, p, p).wait_recv()
            res_ref[:, pl.ds(pl.multiple_of(p * H + h * W, W), W)] = rrecv[h, p]
            back(h, p, y).wait_send()
            d_y(h, p, y).wait_send()
    for p in y_peers:
        for copy in pairs(p, y):
            copy.wait_send()


def local(source_fields, detector_fields, measured, valid_pair, weight_class, absorption):
    NV, NO = lax.axis_size("vox"), lax.axis_size("opt")
    R, DL = measured.shape
    X = absorption.shape[0]
    q = source_fields.shape[0] // R
    B = 2 if DL % 256 == 0 and NV % 4 == 0 else 1
    A = NV // B
    H = DL // B
    W = min(H, 256)
    NH = H // W
    F = 2
    C = NH * B * F
    Q = R // F
    pred_scale = float(np.float32(1.0) / np.sqrt(np.float32(X * NV)))
    grad_scale = float(np.sqrt(np.float32(X * NV)) / np.float32(R * NV * DL * NO))
    bf, f32 = jnp.bfloat16, jnp.float32
    dma = pltpu.SemaphoreType.DMA
    vmem = pl.BlockSpec(memory_space=pltpu.VMEM)
    mu, weighted = pl.pallas_call(
        functools.partial(kernel, A, B, NO, W, pred_scale, grad_scale),
        out_shape=(
            jax.ShapeDtypeStruct((1, X), f32),
            jax.ShapeDtypeStruct((R, DL), f32),
        ),
        in_specs=[pl.BlockSpec(memory_space=pl.ANY)] * 5 + [vmem],
        out_specs=(vmem, vmem),
        scratch_shapes=[
            pltpu.VMEM((A * B, R, B * X), bf),
            pltpu.VMEM((H, B * X), bf),
            pltpu.VMEM((B, R, H), f32),
            pltpu.VMEM((R, DL), jnp.int32),
            pltpu.VMEM((R, DL), jnp.int32),
            pltpu.VMEM((R, DL), bf),
            pltpu.VMEM((B, R, H), bf),
            pltpu.VMEM((1, B * X), f32),
            pltpu.VMEM((B * X, W), bf),
            pltpu.VMEM((C, A, Q, W), f32),
            pltpu.VMEM((C, A, Q, W), bf),
            pltpu.VMEM((ITERS, C, A, Q, W), bf),
            pltpu.VMEM((ITERS, C, 2, Q, W), bf),
            pltpu.VMEM((ITERS, C, A, Q, W), bf),
            pltpu.VMEM((NH, B, R, W), f32),
            pltpu.VMEM((NH, B, R, W), f32),
            pltpu.VMEM((ITERS, B * NO, 1, B * X), f32),
            dma((B,)), dma((B,)),
            dma((NO // 2, B)), dma((NO // 2, B)),
            dma((NO // 2, B)), dma((NO // 2, B)),
            dma((NH, B)), dma((NH, B)),
            dma((3, B)), dma((3, B)),
            dma((NH, B)), dma((NH, B)),
            dma((C, A)), dma((ITERS, C, A)), dma((C,)), dma((ITERS, C)), dma((C, A)),
            dma((C, A)), dma((ITERS, C, A)),
            dma((B * NO,)), dma((ITERS, B * NO)),
            dma((4 + NH,)),
        ],
        compiler_params=pltpu.CompilerParams(
            collective_id=0, has_side_effects=True, vmem_limit_bytes=63 * 1024 * 1024
        ),
    )(
        source_fields.reshape(q, R, X), detector_fields, measured, valid_pair, weight_class,
        absorption.reshape(1, X),
    )
    return mu.reshape(X), weighted


def solution(mesh):
    placed = (
        P("opt", "vox"),
        P("opt", "vox"),
        P("vox", "opt"),
        P("vox", "opt"),
        P("vox", "opt"),
        P("vox"),
    )
    return jax.shard_map(
        local, mesh=mesh, in_specs=placed, out_specs=(P("vox"), P("vox", "opt")), check_vma=False
    )
```
